512 devices in a mesh: leaf: 128 (over y, z, core), blk: 4 (over x).
Axes of the slice: x: 4, y: 4, z: 16, core: 2. Of those that a mesh axis runs over, the one named last changes fastest.
Arguments:
- leaf_basis: bfloat16 [2048, 64, 512], P('leaf'), may hold values from -13 to 13
- leaf_pairing: int32 [128, 16], P('leaf'), may hold values from 0 to 15, each once within a row
- leaf_transfer: float32 [2048, 64, 64], P('leaf'), may hold values from -2 to 2
- inner_transfer: float32 [128, 15, 64, 64], P('leaf'), may hold values from -2 to 2
- upper_transfer: bfloat16 [128, 64, 64], replicated, may hold values from -2 to 2
- coupling: bfloat16 [2048, 16, 64, 64], P('leaf', 'blk'), may hold values from -0.29882812 to 0.29882812
- source_cluster_index: int32 [2048, 16], P('leaf', 'blk'), may hold values from 0 to 2047, as said below
- coupling_slot_mask: int32 [2048, 16], P('leaf', 'blk'), may hold values 0 or 1
Outputs:
- scaled_orthogonal_basis: bfloat16 [2048, 64, 512], P('leaf', None, 'blk')
- inner_cluster_factor: float32 [128, 15, 64, 64], P('leaf')
- parent_upper_factor: float32 [128, 7, 64, 64], P('leaf')
- projected: bfloat16 [2048, 16, 64, 64], P('leaf', 'blk')
- target_row_weight: float32 [2048, 64, 64], P(('leaf', 'blk'))
The draws below stay inside these ranges and needn't reach their ends.
Inputs may be any that keep to these rules, and one draw needn't show every extreme that they name: Each row of leaf_pairing is a permutation of 0 to 15. source_cluster_index[t, s] differs from t by 1 to 8, and by exactly 8 in slot 0.
All inputs are finite; a program needn't handle non-finite values. No bound on the sum of `coupling_slot_mask` on one device may be relied on, other than what follows from the above.
Results may differ from the reference program's by a relative error of at most 0.013.
Values may be sent and summed in bfloat16 or wider, within the bound.
A program may use at most 64 MiB of HBM per device.

```python
import math
import jax
import jax.numpy as jnp
from jax import lax

BASIS_RANK = 64
PANELS = 512
SUBTREE_LEAVES = 16
SLOT_COUNT = 16
LEAF_TOTAL = 2048
COUPLING_REACH = 8
DEPTH = 7
N_LEAF = 128


def draw_leaf_basis(key, part):
    key_scale, key_own, key_common = jax.random.split(jax.random.fold_in(key, 1), 3)
    scales = jnp.exp(jax.random.uniform(key_scale, (LEAF_TOTAL, BASIS_RANK, 1), jnp.float32) * math.log(10.0))
    own_part = jnp.clip(jax.random.normal(key_own, (LEAF_TOTAL, BASIS_RANK, PANELS), jnp.float32), -6.0, 6.0)
    common = jnp.clip(jax.random.normal(key_common, (LEAF_TOTAL, 1, PANELS), jnp.float32), -6.0, 6.0)
    mixture = own_part + 0.7 * common
    return (scales * mixture * (1.0 / math.sqrt(PANELS))).astype(jnp.bfloat16)


def transfer_draw(key, shape):
    width_k = shape[-1]
    noise_part = jnp.clip(jax.random.normal(key, shape, jnp.float32), -6.0, 6.0)
    return 0.75 * jnp.eye(width_k, dtype=jnp.float32) + 0.25 / math.sqrt(width_k) * noise_part


def draw_leaf_transfer(key, part):
    return transfer_draw(jax.random.fold_in(key, 2), (LEAF_TOTAL, BASIS_RANK, BASIS_RANK))


def draw_inner_transfer(key, part):
    return transfer_draw(jax.random.fold_in(key, 3), (N_LEAF, SUBTREE_LEAVES - 1, BASIS_RANK, BASIS_RANK))


def draw_upper_transfer(key, part):
    return transfer_draw(jax.random.fold_in(key, 4), (N_LEAF, BASIS_RANK, BASIS_RANK)).astype(jnp.bfloat16)


def draw_source_cluster_index(key, part):
    random_key_reach, random_key_side = jax.random.split(jax.random.fold_in(key, 5))
    target = jnp.arange(LEAF_TOTAL, dtype=jnp.int32)[:, None]
    column_position = jnp.arange(SLOT_COUNT, dtype=jnp.int32)[None, :]
    reach_sample = jax.random.randint(random_key_reach, (LEAF_TOTAL, SLOT_COUNT), 1, COUPLING_REACH + 1, jnp.int32)
    reach_span = jnp.where(column_position == 0, COUPLING_REACH, reach_sample)
    sweep_direction = 2 * jax.random.randint(random_key_side, (LEAF_TOTAL, SLOT_COUNT), 0, 2, jnp.int32) - 1
    first_try = target + sweep_direction * reach_span
    outside = (first_try < 0) | (first_try >= LEAF_TOTAL)
    return jnp.where(outside, target - sweep_direction * reach_span, first_try).astype(jnp.int32)


def touch_ends(array, own_key, least, high):
    longest = array.shape.index(max(array.shape))
    spots = []
    for shift in (0, 1):
        where = [jax.random.randint(jax.random.fold_in(own_key, axis), (), 0, length) for axis, length in enumerate(array.shape)]
        where[longest] = (where[longest] + shift) % array.shape[longest]
        spots.append(tuple(where))
    return array.at[spots[0]].set(least).at[spots[1]].set(high)


def levels(own_key, extent, shards, low, top_value):
    gain, own = 1.0, jax.random.fold_in(own_key, 6)
    for axis_at, shards_of in shards:
        steps = jnp.exp(jax.random.uniform(jax.random.fold_in(own, axis_at), (shards_of,), jnp.float32, low / len(shards), top_value / len(shards)))
        gain = gain * jnp.repeat(steps, extent[axis_at] // shards_of).reshape([-1 if axis == axis_at else 1 for axis in range(len(extent))])
    return gain


def normal_values(key, extent, scale, limit, cuts=(), held_as=jnp.bfloat16):
    drawn = scale * jax.random.normal(key, extent, jnp.float32)
    if cuts:
        drawn = drawn * levels(key, extent, cuts, -0.22, 0.18)
    return jnp.clip(drawn, -limit, limit).astype(held_as)


def setup_inputs(seed: int = 0) -> dict:
    key_list = jax.random.split(jax.random.key(seed), 9)
    return {
        "leaf_basis": draw_leaf_basis(jax.random.fold_in(key_list[8], 71), 0),
        "leaf_pairing": jax.vmap(lambda own: jax.random.permutation(own, SUBTREE_LEAVES))(jax.random.split(key_list[1], N_LEAF)).reshape((N_LEAF, SUBTREE_LEAVES)).astype(jnp.int32),
        "leaf_transfer": draw_leaf_transfer(jax.random.fold_in(key_list[8], 71), 0),
        "inner_transfer": draw_inner_transfer(jax.random.fold_in(key_list[8], 71), 0),
        "upper_transfer": draw_upper_transfer(jax.random.fold_in(key_list[8], 71), 0),
        "coupling": normal_values(key_list[5], (LEAF_TOTAL, SLOT_COUNT, BASIS_RANK, BASIS_RANK), 0.05, 0.29882812, ((0, 128), (1, 4))),
        "source_cluster_index": draw_source_cluster_index(jax.random.fold_in(key_list[8], 71), 0),
        "coupling_slot_mask": touch_ends((jax.random.randint(key_list[7], (LEAF_TOTAL, SLOT_COUNT), 0, 4) < 3).astype(jnp.int32), jax.random.fold_in(key_list[7], 1), 0, 1),
    }


highest_precision = lax.Precision.HIGHEST

def carry_up(transfer, gram_in):
    left_part = jnp.einsum('nba,nbc->nac', transfer, gram_in, precision=highest_precision)
    return jnp.einsum('nac,ncd->nad', left_part, transfer, precision=highest_precision)

def pair_sum(term_stack):
    node_count = term_stack.shape[0] // 2
    paired = term_stack.reshape(node_count, 2, term_stack.shape[1], term_stack.shape[2])
    return paired[:, 0] + paired[:, 1]

def triangle_of(gram_in):
    return jnp.swapaxes(jnp.linalg.cholesky(gram_in), -1, -2)

def inverse_of(factor):
    identity = jnp.broadcast_to(jnp.eye(factor.shape[-1], dtype=factor.dtype), factor.shape)
    return lax.linalg.triangular_solve(factor, identity, left_side=True, lower=False)

def local_tree(gram_leaf, leaf_order, leaf_moves, inner_moves):
    ordered_gram = jnp.take(gram_leaf, leaf_order, axis=0)
    ordered_move = jnp.take(leaf_moves, leaf_order, axis=0)
    level_gram = pair_sum(carry_up(ordered_move, ordered_gram))
    level_list = [level_gram]
    slot_offset = 0
    while level_gram.shape[0] > 1:
        node_count = level_gram.shape[0]
        level_gram = pair_sum(carry_up(inner_moves[slot_offset:slot_offset + node_count], level_gram))
        slot_offset = slot_offset + node_count
        level_list.append(level_gram)
    node_grams = jnp.concatenate(level_list, axis=0)
    root_term = carry_up(inner_moves[slot_offset:slot_offset + 1], level_gram)[0]
    return (node_grams, root_term)

def reference(leaf_basis, leaf_pairing, leaf_transfer, inner_transfer, upper_transfer, coupling, source_cluster_index, coupling_slot_mask):
    basis_blocks = leaf_basis.reshape(N_LEAF, SUBTREE_LEAVES, BASIS_RANK, PANELS)
    move_blocks = leaf_transfer.reshape(N_LEAF, SUBTREE_LEAVES, BASIS_RANK, BASIS_RANK)

    def one_block(operands):
        basis_here, order_here, moves_here, inner_here = operands
        wide_basis = basis_here.astype(jnp.float32)
        gram_leaf = jnp.einsum('lkp,ljp->lkj', wide_basis, wide_basis, precision=highest_precision)
        node_grams, root_term = local_tree(gram_leaf, order_here, moves_here, inner_here)
        leaf_factor = triangle_of(gram_leaf)
        weights = (math.sqrt(PANELS) * inverse_of(leaf_factor)).astype(jnp.bfloat16)
        q_here = jnp.einsum('lkj,lkp->ljp', weights.astype(jnp.float32), wide_basis, precision=highest_precision).astype(jnp.bfloat16)
        return (triangle_of(node_grams), root_term, leaf_factor, q_here)
    inner_cluster_factor, root_terms, leaf_factors, q_blocks = lax.map(one_block, (basis_blocks, leaf_pairing, move_blocks, inner_transfer))
    upper_wide = upper_transfer.astype(jnp.float32)
    level_gram = pair_sum(root_terms)
    factor_levels = []
    for tree_level in range(1, DEPTH + 1):
        if tree_level > 1:
            stride = 2 ** (tree_level - 1)
            moves_up = upper_wide.reshape(N_LEAF // stride, stride, BASIS_RANK, BASIS_RANK)[:, stride // 2]
            level_gram = pair_sum(carry_up(moves_up, level_gram))
        factor_levels.append(jnp.repeat(triangle_of(level_gram), 2 ** tree_level, axis=0))
    parent_upper_factor = jnp.stack(factor_levels, axis=1)
    lower_factor_half = leaf_factors.reshape(LEAF_TOTAL, BASIS_RANK, BASIS_RANK).astype(jnp.bfloat16)

    def single_coupling(operands):
        target_low, blocks_here, sources_here, mask_here = operands
        half_proj = jnp.einsum('tab,tsbc->tsac', target_low.astype(jnp.float32), blocks_here.astype(jnp.float32), precision=highest_precision).astype(jnp.bfloat16)
        source_low = jnp.take(lower_factor_half, sources_here, axis=0)
        full_proj = jnp.einsum('tsac,tsdc->tsad', half_proj.astype(jnp.float32), source_low.astype(jnp.float32), precision=highest_precision)
        projected = (full_proj * mask_here.astype(jnp.float32)[:, :, None, None]).astype(jnp.bfloat16)
        wide_projection = projected.astype(jnp.float32)
        target_row_weight = jnp.einsum('lfdv,lfrv->ldr', wide_projection, wide_projection, precision=highest_precision) * (1.0 / (SLOT_COUNT * BASIS_RANK))
        return (projected, target_row_weight)
    projected, target_row_weight = lax.map(single_coupling, (lower_factor_half.reshape(N_LEAF, SUBTREE_LEAVES, BASIS_RANK, BASIS_RANK), coupling.reshape(N_LEAF, SUBTREE_LEAVES, SLOT_COUNT, BASIS_RANK, BASIS_RANK), source_cluster_index.reshape(N_LEAF, SUBTREE_LEAVES, SLOT_COUNT), coupling_slot_mask.reshape(N_LEAF, SUBTREE_LEAVES, SLOT_COUNT)))
    scaled_orthogonal_basis = q_blocks.reshape(LEAF_TOTAL, BASIS_RANK, PANELS)
    return (scaled_orthogonal_basis, inner_cluster_factor, parent_upper_factor, projected.reshape(LEAF_TOTAL, SLOT_COUNT, BASIS_RANK, BASIS_RANK), target_row_weight.reshape(LEAF_TOTAL, BASIS_RANK, BASIS_RANK))
```

```python
import functools
import math

import jax
import jax.numpy as jnp
from jax import lax
from jax.experimental import pallas as pl
from jax.experimental.pallas import tpu as pltpu
from jax.sharding import PartitionSpec as P

F32 = jnp.float32
BF16 = jnp.bfloat16
VMEM = pltpu.VMEM
SMEM = pltpu.SMEM


def split(x):
    high = x.astype(BF16)
    return high, (x - high.astype(F32)).astype(BF16)


def dot_nn(a, b):
    return lax.dot_general(a, b, (((1,), (0,)), ((), ())), preferred_element_type=F32)


def dot_nt(a, b):
    return lax.dot_general(a, b, (((1,), (1,)), ((), ())), preferred_element_type=F32)


def dot_tn(a, b):
    return lax.dot_general(a, b, (((0,), (0,)), ((), ())), preferred_element_type=F32)


def carry(move, gram):
    move_h, move_l = move
    gram_h, gram_l = split(gram)
    right = dot_nn(gram_h, move_h) + dot_nn(gram_l, move_h)
    if move_l is not None:
        right = right + dot_nn(gram_h, move_l)
    right_h, right_l = split(right)
    out = dot_tn(move_h, right_h) + dot_tn(move_h, right_l)
    if move_l is not None:
        out = out + dot_tn(move_l, right_h)
    return out


def panel_chain(panel, start):
    count, rows, _ = panel.shape
    sub = lax.broadcasted_iota(jnp.int32, (1, rows, 128), 1)
    scale = jnp.zeros((count, rows, 128), F32)
    for r in range(rows):
        col = jnp.broadcast_to(panel[:, :, start + r : start + r + 1], panel.shape)
        inv = lax.rsqrt(col[:, r : r + 1, :])
        outer = jnp.where(sub > r, col, 0.0) * panel[:, r : r + 1, :]
        panel = panel - outer * (inv * inv)
        scale = jnp.where(sub == r, inv, scale)
    return panel * scale


def panel_ahead(panel, start):
    count, rows, _ = panel.shape
    sub = lax.broadcasted_iota(jnp.int32, (1, rows, 128), 1)
    scale = jnp.zeros((count, rows, 128), F32)
    cols = [
        jnp.broadcast_to(panel[:, :, start + r : start + r + 1], panel.shape) for r in range(rows)
    ]
    for r in range(rows):
        inv = lax.rsqrt(cols[r][:, r : r + 1, :])
        mult = jnp.where(sub > r, cols[r], 0.0) * (inv * inv)
        panel = panel - mult * panel[:, r : r + 1, :]
        for t in range(r + 1, rows):
            cols[t] = cols[t] - mult * cols[t][:, r : r + 1, :]
        scale = jnp.where(sub == r, inv, scale)
    return panel * scale


def factor(work, done, first, count, rows, eliminate):
    size = work.shape[1]
    last = first + count
    for k in range(0, size, rows):
        panel = eliminate(work[first:last, k : k + rows, :], k)
        done[first:last, k : k + rows, :] = panel
        if k + rows < size:
            high, low = split(panel)
            left = jnp.concatenate([high, low, high], axis=1)
            right = jnp.concatenate([high, high, low], axis=1)
            for i in range(count):
                down = dot_tn(left[i], right[i])
                work[first + i, k + rows : size, :] = (
                    work[first + i, k + rows : size, :] - down[k + rows : size, :]
                )


def upper_mask(size):
    return lax.broadcasted_iota(jnp.int32, (size, size), 0) <= lax.broadcasted_iota(
        jnp.int32, (size, size), 1
    )


def eye(size):
    return (
        lax.broadcasted_iota(jnp.int32, (size, size), 0)
        == lax.broadcasted_iota(jnp.int32, (size, size), 1)
    ).astype(F32)


def tree_kernel(pairing, basis, leaf_move, inner_move, q_out, inner_out, root_out, low_out, work, done):
    leaves, size, panels = basis.shape
    inner = inner_move.shape[0]
    part = q_out.shape[2]
    identity = eye(size)
    for i in range(leaves + inner):
        work[i, :, size : 2 * size] = identity
    for i in range(leaves):
        work[i, :, 0:size] = dot_nt(basis[i], basis[i])
    for m in range(leaves // 2):
        a, b = pairing[0, 2 * m], pairing[0, 2 * m + 1]
        work[leaves + m, :, 0:size] = carry(split(leaf_move[a]), work[a, :, 0:size]) + carry(
            split(leaf_move[b]), work[b, :, 0:size]
        )
    below, count = 0, leaves // 2
    while count > 1:
        for m in range(count // 2):
            a = below + 2 * m
            work[leaves + below + count + m, :, 0:size] = carry(
                split(inner_move[a]), work[leaves + a, :, 0:size]
            ) + carry(split(inner_move[a + 1]), work[leaves + a + 1, :, 0:size])
        below, count = below + count, count // 2
    root_out[...] = carry(split(inner_move[inner - 1]), work[leaves + inner - 1, :, 0:size])
    factor(work, done, 0, leaves + inner, 16, panel_chain)
    keep = upper_mask(size)
    for i in range(inner):
        inner_out[i] = jnp.where(keep, done[leaves + i, :, 0:size], 0.0)
    begin = pl.multiple_of(lax.axis_index("blk") * part, part)
    for i in range(leaves):
        low_out[i] = jnp.where(keep, done[i, :, 0:size], 0.0).astype(BF16)
        weights = (math.sqrt(panels) * done[i, :, size : 2 * size]).astype(BF16)
        q_out[i] = dot_nn(weights, basis[i, :, pl.ds(begin, part)]).astype(BF16)


def pack(matrix):
    half = matrix.shape[0] // 2
    return jnp.concatenate([matrix[:half], matrix[half:]], axis=1)


def unpack(packed):
    half = packed.shape[1] // 2
    return jnp.concatenate([packed[:, :half], packed[:, half:]], axis=0)


def link_kernel(
    index,
    mask,
    root,
    moves,
    low,
    coupling,
    upper_out,
    projected,
    weight_out,
    extended,
    half_ref,
    send,
    recv,
    row_send,
    row_recv,
    work,
    done,
    send_sem,
    recv_sem,
    halo_send_sem,
    halo_recv_sem,
    row_send_sem,
    row_recv_sem,
):
    leaves, slots, size, _ = coupling.shape
    halo = leaves // 2
    n_leaf, blocks = lax.axis_size("leaf"), lax.axis_size("blk")
    me, blk = lax.axis_index("leaf"), lax.axis_index("blk")
    after, before = lax.rem(me + 1, n_leaf), lax.rem(me + n_leaf - 1, n_leaf)
    depth = upper_out.shape[0]

    def flipped(apart):
        out, bit = me, 1
        while bit <= apart:
            if apart & bit:
                out = out + bit - 2 * bit * lax.rem(out // bit, 2)
            bit *= 2
        return out

    groups = [(1,)] + [(2 << (2 * g), 4 << (2 * g), 6 << (2 * g)) for g in range((depth - 1) // 2)]
    barrier = pltpu.get_barrier_semaphore()
    total = 0
    for group in groups:
        for apart in group:
            pl.semaphore_signal(barrier, 1, device_id={"leaf": flipped(apart)})
            total += 1
    for peer in (after, before):
        pl.semaphore_signal(barrier, 1, device_id={"leaf": peer})
        total += 1
    for d in range(1, blocks):
        pl.semaphore_signal(barrier, 1, device_id={"blk": lax.rem(blk + d, blocks)})
        total += 1
    pl.semaphore_wait(barrier, total)

    slot_of, used = {}, [0, 0]

    def start_exchange(step, terms):
        firsts = []
        for term in terms:
            send[used[0]] = pack(term)
            firsts.append(used[0])
            used[0] += 1
        started = []
        for j, apart in enumerate(groups[step]):
            parts = firsts if j == 0 else firsts[-1:]
            for source in parts:
                at = used[1]
                used[1] += 1
                copy = pltpu.make_async_remote_copy(
                    src_ref=send.at[source],
                    dst_ref=recv.at[at],
                    send_sem=send_sem.at[at],
                    recv_sem=recv_sem.at[at],
                    device_id={"leaf": flipped(apart)},
                )
                copy.start()
                started.append((copy, source, at))
        return started

    def finish_exchange(started):
        sums = {}
        for copy, source, at in started:
            copy.wait_recv()
            sums[source] = sums.get(source, send[source]) + recv[at]
        return [unpack(sums[s]) for s in sorted(sums)]

    grams = []

    def next_terms(gram):
        level = len(grams)
        near = moves[level - 1]
        far = split(dot_nn(near, moves[level]))
        return [carry((near, None), gram), carry(far, gram)]

    going = [start_exchange(0, [root[...]])]
    for i in range(leaves):
        extended[halo + i] = low[i]
    halo_copies = []
    for j, (peer, source, target) in enumerate(
        ((after, halo + leaves - halo, 0), (before, halo, halo + leaves))
    ):
        copy = pltpu.make_async_remote_copy(
            src_ref=extended.at[pl.ds(source, halo)],
            dst_ref=extended.at[pl.ds(target, halo)],
            send_sem=halo_send_sem.at[j],
            recv_sem=halo_recv_sem.at[j],
            device_id={"leaf": peer},
        )
        copy.start()
        halo_copies.append(copy)

    for t in range(leaves):
        for s in range(slots):
            half_ref[t, s] = dot_nn(low[t], coupling[t, s]).astype(BF16)

    grams += finish_exchange(going[-1])
    going.append(start_exchange(1, next_terms(grams[-1])))
    for copy in halo_copies:
        copy.wait_recv()

    per = leaves // blocks
    base = me * leaves - halo
    row_scale = 1.0 / (slots * blocks * size)
    row_copies = []
    own_rows = []
    for d in range(1, blocks + 1):
        peer = lax.rem(blk + d, blocks)
        for i in range(per):
            t = peer * per + i
            rows = None
            for s in range(slots):
                source = jnp.clip(index[t, s] - base, 0, leaves + 2 * halo - 1)
                full = dot_nt(half_ref[t, s], extended[source])
                value = (full * mask[t, s].astype(F32)).astype(BF16)
                projected[t, s] = value
                term = dot_nt(value, value)
                rows = term if rows is None else rows + term
            if d < blocks:
                row_send[d - 1, i] = (rows * row_scale).astype(BF16)
            else:
                own_rows.append(rows * row_scale)
        if d < blocks:
            copy = pltpu.make_async_remote_copy(
                src_ref=row_send.at[d - 1],
                dst_ref=row_recv.at[d - 1],
                send_sem=row_send_sem.at[d - 1],
                recv_sem=row_recv_sem.at[d - 1],
                device_id={"blk": peer},
            )
            copy.start()
            row_copies.append(copy)
        if d < len(groups) - 1:
            grams += finish_exchange(going[-1])
            going.append(start_exchange(d + 1, next_terms(grams[-1])))
    for copy in row_copies:
        copy.wait_recv()
    for i in range(per):
        rows = own_rows[i]
        for d in range(blocks - 1):
            rows = rows + row_recv[d, i].astype(F32)
        weight_out[i] = rows
    grams += finish_exchange(going[-1])

    for i in range(depth):
        work[i, :, 0:size] = grams[i]
        work[i, :, size : 2 * size] = jnp.zeros((size, size), F32)
    factor(work, done, 0, depth, 8, panel_ahead)
    keep = upper_mask(size)
    for i in range(depth):
        upper_out[i] = jnp.where(keep, done[i, :, 0:size], 0.0)
    for started in going:
        for copy, _, _ in started:
            copy.wait_send()
    for copy in halo_copies + row_copies:
        copy.wait_send()


def local(
    leaf_basis,
    leaf_pairing,
    leaf_transfer,
    inner_transfer,
    upper_transfer,
    coupling,
    source_cluster_index,
    coupling_slot_mask,
):
    leaves, size, panels = leaf_basis.shape
    inner = inner_transfer.shape[1]
    n_leaf, blocks = lax.axis_size("leaf"), lax.axis_size("blk")
    depth = n_leaf.bit_length() - 1
    slots = coupling.shape[1]
    part = panels // blocks
    vmem = pl.BlockSpec(memory_space=VMEM)
    smem = pl.BlockSpec(memory_space=SMEM)

    q, inner_factor, root, low = pl.pallas_call(
        tree_kernel,
        out_shape=(
            jax.ShapeDtypeStruct((leaves, size, part), BF16),
            jax.ShapeDtypeStruct((inner, size, size), F32),
            jax.ShapeDtypeStruct((size, size), F32),
            jax.ShapeDtypeStruct((leaves, size, size), BF16),
        ),
        in_specs=[smem, vmem, vmem, vmem],
        out_specs=(vmem,) * 4,
        scratch_shapes=[
            VMEM((leaves + inner, size, 2 * size), F32),
            VMEM((leaves + inner, size, 2 * size), F32),
        ],
        compiler_params=pltpu.CompilerParams(vmem_limit_bytes=40 * 2**20),
    )(leaf_pairing, leaf_basis, leaf_transfer, inner_transfer[0])

    me = lax.axis_index("leaf")
    level = jnp.arange(1, depth, dtype=jnp.int32)
    owner = (me >> level << level) + (1 << (level - 1))
    choose = (owner[:, None] == jnp.arange(n_leaf, dtype=jnp.int32)[None, :]).astype(BF16)
    moves = jnp.einsum("rn,nba->rba", choose, upper_transfer, preferred_element_type=F32).astype(
        BF16
    )

    n_recv = 1 + 4 * ((depth - 1) // 2)
    n_send = 1 + 2 * ((depth - 1) // 2)
    upper_factor, projected, row_weight = pl.pallas_call(
        link_kernel,
        out_shape=(
            jax.ShapeDtypeStruct((depth, size, size), F32),
            jax.ShapeDtypeStruct(coupling.shape, BF16),
            jax.ShapeDtypeStruct((leaves // blocks, size, size), F32),
        ),
        in_specs=[smem, smem, vmem, vmem, vmem, vmem],
        out_specs=(vmem,) * 3,
        scratch_shapes=[
            VMEM((2 * leaves, size, size), BF16),
            VMEM((leaves, slots, size, size), BF16),
            VMEM((n_send, size // 2, 2 * size), F32),
            VMEM((n_recv, size // 2, 2 * size), F32),
            VMEM((blocks - 1, leaves // blocks, size, size), BF16),
            VMEM((blocks - 1, leaves // blocks, size, size), BF16),
            VMEM((depth, size, 2 * size), F32),
            VMEM((depth, size, 2 * size), F32),
            pltpu.SemaphoreType.DMA((n_recv,)),
            pltpu.SemaphoreType.DMA((n_recv,)),
            pltpu.SemaphoreType.DMA((2,)),
            pltpu.SemaphoreType.DMA((2,)),
            pltpu.SemaphoreType.DMA((blocks - 1,)),
            pltpu.SemaphoreType.DMA((blocks - 1,)),
        ],
        compiler_params=pltpu.CompilerParams(
            collective_id=0, has_side_effects=True, vmem_limit_bytes=40 * 2**20
        ),
    )(source_cluster_index, coupling_slot_mask, root, moves, low, coupling)
    return (q, inner_factor[None], upper_factor[None], projected, row_weight)


def solution(mesh):
    placed = (
        P("leaf", None, None),
        P("leaf", None),
        P("leaf", None, None),
        P("leaf", None, None, None),
        P(),
        P("leaf", "blk", None, None),
        P("leaf", "blk"),
        P("leaf", "blk"),
    )
    return jax.shard_map(
        local,
        mesh=mesh,
        in_specs=placed,
        out_specs=(
            P("leaf", None, "blk"),
            P("leaf", None, None, None),
            P("leaf", None, None, None),
            P("leaf", "blk", None, None),
            P(("leaf", "blk"), None, None),
        ),
        check_vma=False,
    )
```

```python
import functools
import math

import jax
import jax.numpy as jnp
from jax import lax
from jax.experimental import pallas as pl
from jax.experimental.pallas import tpu as pltpu
from jax.sharding import PartitionSpec as P

F32 = jnp.float32
BF16 = jnp.bfloat16
VMEM = pltpu.VMEM
SMEM = pltpu.SMEM


def split(x):
    high = x.astype(BF16)
    return high, (x - high.astype(F32)).astype(BF16)


def dot_nn(a, b):
    return lax.dot_general(a, b, (((1,), (0,)), ((), ())), preferred_element_type=F32)


def dot_nt(a, b):
    return lax.dot_general(a, b, (((1,), (1,)), ((), ())), preferred_element_type=F32)


def dot_tn(a, b):
    return lax.dot_general(a, b, (((0,), (0,)), ((), ())), preferred_element_type=F32)


def carry(move, gram):
    move_h, move_l = move
    gram_h, gram_l = split(gram)
    right = dot_nn(gram_h, move_h) + dot_nn(gram_l, move_h)
    if move_l is not None:
        right = right + dot_nn(gram_h, move_l)
    right_h, right_l = split(right)
    out = dot_tn(move_h, right_h) + dot_tn(move_h, right_l)
    if move_l is not None:
        out = out + dot_tn(move_l, right_h)
    return out


def panel_chain(panel, start):
    count, rows, _ = panel.shape
    sub = lax.broadcasted_iota(jnp.int32, (1, rows, 128), 1)
    scale = jnp.zeros((count, rows, 128), F32)
    for r in range(rows):
        col = jnp.broadcast_to(panel[:, :, start + r : start + r + 1], panel.shape)
        inv = lax.rsqrt(col[:, r : r + 1, :])
        outer = jnp.where(sub > r, col, 0.0) * panel[:, r : r + 1, :]
        panel = panel - outer * (inv * inv)
        scale = jnp.where(sub == r, inv, scale)
    return panel * scale


def panel_ahead(panel, start):
    count, rows, _ = panel.shape
    sub = lax.broadcasted_iota(jnp.int32, (1, rows, 128), 1)
    scale = jnp.zeros((count, rows, 128), F32)
    cols = [
        jnp.broadcast_to(panel[:, :, start + r : start + r + 1], panel.shape) for r in range(rows)
    ]
    for r in range(rows):
        inv = lax.rsqrt(cols[r][:, r : r + 1, :])
        mult = jnp.where(sub > r, cols[r], 0.0) * (inv * inv)
        panel = panel - mult * panel[:, r : r + 1, :]
        for t in range(r + 1, rows):
            cols[t] = cols[t] - mult * cols[t][:, r : r + 1, :]
        scale = jnp.where(sub == r, inv, scale)
    return panel * scale


def factor_panel(work, done, first, count, rows, k, eliminate):
    size = work.shape[1]
    last = first + count
    panel = eliminate(work[first:last, k : k + rows, :], k)
    done[first:last, k : k + rows, :] = panel
    if k + rows < size:
        high, low = split(panel)
        left = jnp.concatenate([high, low, high], axis=1)
        right = jnp.concatenate([high, high, low], axis=1)
        for i in range(count):
            down = dot_tn(left[i], right[i])
            work[first + i, k + rows : size, :] = (
                work[first + i, k + rows : size, :] - down[k + rows : size, :]
            )


def upper_mask(size):
    return lax.broadcasted_iota(jnp.int32, (size, size), 0) <= lax.broadcasted_iota(
        jnp.int32, (size, size), 1
    )


def eye(size):
    return (
        lax.broadcasted_iota(jnp.int32, (size, size), 0)
        == lax.broadcasted_iota(jnp.int32, (size, size), 1)
    ).astype(F32)


def pack(matrix):
    half = matrix.shape[0] // 2
    return jnp.concatenate([matrix[:half], matrix[half:]], axis=1)


def unpack(packed):
    half = packed.shape[1] // 2
    return jnp.concatenate([packed[:, :half], packed[:, half:]], axis=0)


def tree_kernel(
    pairing_hbm,
    basis_hbm,
    leaf_move_hbm,
    inner_move_hbm,
    moves_hbm,
    coupling_hbm,
    index_hbm,
    mask_hbm,
    q_hbm,
    inner_hbm,
    gram_hbm,
    projected_hbm,
    weight_hbm,
    q_out,
    inner_out,
    gram_out,
    projected,
    weight_out,
    pairing,
    basis,
    leaf_move,
    inner_move,
    moves,
    coupling,
    index,
    mask,
    work,
    done,
    extended,
    half_ref,
    send,
    recv,
    row_send,
    row_recv,
    in_sem,
    out_sem,
    send_sem,
    recv_sem,
    halo_send_sem,
    halo_recv_sem,
    row_send_sem,
    row_recv_sem,
):
    leaves, size, panels = basis.shape
    inner = inner_move.shape[0]
    slots = coupling.shape[1]
    part = q_out.shape[2]
    halo = leaves // 2
    n_leaf, blocks = lax.axis_size("leaf"), lax.axis_size("blk")
    me, blk = lax.axis_index("leaf"), lax.axis_index("blk")
    after, before = lax.rem(me + 1, n_leaf), lax.rem(me + n_leaf - 1, n_leaf)
    depth = gram_out.shape[0]

    loads = []
    for j, (source, target) in enumerate(
        (
            (basis_hbm, basis),
            (pairing_hbm, pairing),
            (leaf_move_hbm, leaf_move),
            (inner_move_hbm, inner_move),
            (moves_hbm, moves),
            (coupling_hbm, coupling),
            (index_hbm, index),
            (mask_hbm, mask),
        )
    ):
        load = pltpu.make_async_copy(source, target, in_sem.at[j])
        load.start()
        loads.append(load)

    stores = []

    def store_out(source, target):
        store = pltpu.make_async_copy(source, target, out_sem.at[len(stores)])
        store.start()
        stores.append(store)

    def flipped(apart):
        out, bit = me, 1
        while bit <= apart:
            if apart & bit:
                out = out + bit - 2 * bit * lax.rem(out // bit, 2)
            bit *= 2
        return out

    groups = [(1,)] + [(2 << (2 * g), 4 << (2 * g), 6 << (2 * g)) for g in range((depth - 1) // 2)]
    barrier = pltpu.get_barrier_semaphore()
    total = 0
    for group in groups:
        for apart in group:
            pl.semaphore_signal(barrier, 1, device_id={"leaf": flipped(apart)})
            total += 1
    for peer in (after, before):
        pl.semaphore_signal(barrier, 1, device_id={"leaf": peer})
        total += 1
    for d in range(1, blocks):
        pl.semaphore_signal(barrier, 1, device_id={"blk": lax.rem(blk + d, blocks)})
        total += 1

    used = [0, 0]

    def start_exchange(step, terms):
        firsts = []
        for term in terms:
            send[used[0]] = pack(term)
            firsts.append(used[0])
            used[0] += 1
        started = []
        for j, apart in enumerate(groups[step]):
            parts = firsts if j == 0 else firsts[-1:]
            for source in parts:
                at = used[1]
                used[1] += 1
                copy = pltpu.make_async_remote_copy(
                    src_ref=send.at[source],
                    dst_ref=recv.at[at],
                    send_sem=send_sem.at[at],
                    recv_sem=recv_sem.at[at],
                    device_id={"leaf": flipped(apart)},
                )
                copy.start()
                started.append((copy, source, at))
        return started

    def finish_exchange(started):
        sums = {}
        for copy, source, at in started:
            copy.wait_recv()
            sums[source] = sums.get(source, send[source]) + recv[at]
        return [unpack(sums[s]) for s in sorted(sums)]

    grams, going = [], []

    def advance():
        grams.extend(finish_exchange(going[-1]))
        if len(going) < len(groups):
            level = len(grams)
            near = moves[level - 1]
            far = split(dot_nn(near, moves[level]))
            terms = [carry((near, None), grams[-1]), carry(far, grams[-1])]
            going.append(start_exchange(len(going), terms))

    identity = eye(size)
    for i in range(leaves + inner):
        work[i, :, size : 2 * size] = identity
    loads[0].wait()
    for i in range(leaves):
        work[i, :, 0:size] = dot_nt(basis[i], basis[i])
    for j in (1, 2, 3):
        loads[j].wait()
    for m in range(leaves // 2):
        a, b = pairing[0, 2 * m], pairing[0, 2 * m + 1]
        work[leaves + m, :, 0:size] = carry(split(leaf_move[a]), work[a, :, 0:size]) + carry(
            split(leaf_move[b]), work[b, :, 0:size]
        )
    below, count = 0, leaves // 2
    while count > 1:
        for m in range(count // 2):
            a = below + 2 * m
            work[leaves + below + count + m, :, 0:size] = carry(
                split(inner_move[a]), work[leaves + a, :, 0:size]
            ) + carry(split(inner_move[a + 1]), work[leaves + a + 1, :, 0:size])
        below, count = below + count, count // 2
    root = carry(split(inner_move[inner - 1]), work[leaves + inner - 1, :, 0:size])
    pl.semaphore_wait(barrier, total)
    going.append(start_exchange(0, [root]))
    for j in (4, 5, 6, 7):
        loads[j].wait()

    rows = 16
    for k in range(0, size, rows):
        factor_panel(work, done, 0, leaves + inner, rows, k, panel_chain)
        if k + rows < size:
            advance()

    keep = upper_mask(size)
    for i in range(leaves):
        extended[halo + i] = jnp.where(keep, done[i, :, 0:size], 0.0).astype(BF16)
    halo_copies = []
    for j, (peer, source, target) in enumerate(((after, leaves, 0), (before, halo, halo + leaves))):
        copy = pltpu.make_async_remote_copy(
            src_ref=extended.at[pl.ds(source, halo)],
            dst_ref=extended.at[pl.ds(target, halo)],
            send_sem=halo_send_sem.at[j],
            recv_sem=halo_recv_sem.at[j],
            device_id={"leaf": peer},
        )
        copy.start()
        halo_copies.append(copy)

    for t in range(leaves):
        for s in range(slots):
            half_ref[t, s] = dot_nn(extended[halo + t], coupling[t, s]).astype(BF16)
    begin = pl.multiple_of(blk * part, part)
    for i in range(leaves):
        weights = (math.sqrt(panels) * done[i, :, size : 2 * size]).astype(BF16)
        q_out[i] = dot_nn(weights, basis[i, :, pl.ds(begin, part)]).astype(BF16)
    for i in range(inner):
        inner_out[i] = jnp.where(keep, done[leaves + i, :, 0:size], 0.0)
    store_out(q_out, q_hbm)
    store_out(inner_out, inner_hbm)

    for copy in halo_copies:
        copy.wait_recv()
    per = leaves // blocks
    base = me * leaves - halo
    row_scale = 1.0 / (slots * blocks * size)
    row_copies = []
    own_rows = []
    for d in range(1, blocks + 1):
        peer = lax.rem(blk + d, blocks)
        for i in range(per):
            t = peer * per + i
            square = None
            for s in range(slots):
                source = jnp.clip(index[s, t] - base, 0, leaves + 2 * halo - 1)
                full = dot_nt(half_ref[t, s], extended[source])
                value = (full * mask[s, t].astype(F32)).astype(BF16)
                projected[t, s] = value
                term = dot_nt(value, value)
                square = term if square is None else square + term
            if d < blocks:
                row_send[d - 1, i] = (square * row_scale).astype(BF16)
            else:
                own_rows.append(square * row_scale)
        if d < blocks:
            copy = pltpu.make_async_remote_copy(
                src_ref=row_send.at[d - 1],
                dst_ref=row_recv.at[d - 1],
                send_sem=row_send_sem.at[d - 1],
                recv_sem=row_recv_sem.at[d - 1],
                device_id={"blk": peer},
            )
            copy.start()
            row_copies.append(copy)
    store_out(projected, projected_hbm)
    advance()
    for i in range(depth):
        gram_out[i] = grams[i]
    store_out(gram_out, gram_hbm)
    for copy in row_copies:
        copy.wait_recv()
    for i in range(per):
        square = own_rows[i]
        for d in range(blocks - 1):
            square = square + row_recv[d, i].astype(F32)
        weight_out[i] = square
    store_out(weight_out, weight_hbm)
    for started in going:
        for copy, _, _ in started:
            copy.wait_send()
    for copy in halo_copies + row_copies:
        copy.wait_send()
    for store in stores:
        store.wait()


def last_kernel(
    gram, q, inner, projected, weight, upper_out, q_out, inner_out, projected_out, weight_out, work, done, sem
):
    depth, size, _ = gram.shape
    stores = []
    for j, (source, target) in enumerate(
        ((projected, projected_out), (q, q_out), (inner, inner_out), (weight, weight_out))
    ):
        store = pltpu.make_async_copy(source, target, sem.at[j])
        store.start()
        stores.append(store)
    for i in range(depth):
        work[i, :, 0:size] = gram[i]
        work[i, :, size : 2 * size] = jnp.zeros((size, size), F32)
    rows = 8
    for k in range(0, size, rows):
        factor_panel(work, done, 0, depth, rows, k, panel_ahead)
    keep = upper_mask(size)
    for i in range(depth):
        upper_out[i] = jnp.where(keep, done[i, :, 0:size], 0.0)
    for store in stores:
        store.wait()


def local(
    leaf_basis,
    leaf_pairing,
    leaf_transfer,
    inner_transfer,
    upper_transfer,
    coupling,
    source_cluster_index,
    coupling_slot_mask,
):
    leaves, size, panels = leaf_basis.shape
    inner = inner_transfer.shape[1]
    n_leaf, blocks = lax.axis_size("leaf"), lax.axis_size("blk")
    depth = n_leaf.bit_length() - 1
    slots = coupling.shape[1]
    part = panels // blocks
    vmem = pl.BlockSpec(memory_space=VMEM)
    anywhere = pl.BlockSpec(memory_space=pl.ANY)

    me = lax.axis_index("leaf")
    level = jnp.arange(1, depth, dtype=jnp.int32)
    owner = (me >> level << level) + (1 << (level - 1))
    choose = (owner[:, None] == jnp.arange(n_leaf, dtype=jnp.int32)[None, :]).astype(BF16)
    moves = jnp.einsum("rn,nba->rba", choose, upper_transfer, preferred_element_type=F32).astype(
        BF16
    )

    n_recv = 1 + 4 * ((depth - 1) // 2)
    n_send = 1 + 2 * ((depth - 1) // 2)
    q_shape = jax.ShapeDtypeStruct((leaves, size, part), BF16)
    inner_shape = jax.ShapeDtypeStruct((inner, size, size), F32)
    upper_shape = jax.ShapeDtypeStruct((depth, size, size), F32)
    projected_shape = jax.ShapeDtypeStruct(coupling.shape, BF16)
    weight_shape = jax.ShapeDtypeStruct((leaves // blocks, size, size), F32)
    q, inner_factor, upper_gram, projected, row_weight = pl.pallas_call(
        tree_kernel,
        out_shape=(q_shape, inner_shape, upper_shape, projected_shape, weight_shape),
        in_specs=[anywhere] * 8,
        out_specs=(anywhere,) * 5,
        scratch_shapes=[
            VMEM(q_shape.shape, BF16),
            VMEM(inner_shape.shape, F32),
            VMEM(upper_shape.shape, F32),
            VMEM(coupling.shape, BF16),
            VMEM(weight_shape.shape, F32),
            SMEM((1, leaves), jnp.int32),
            VMEM((leaves, size, panels), BF16),
            VMEM((leaves, size, size), F32),
            VMEM((inner, size, size), F32),
            VMEM((depth - 1, size, size), BF16),
            VMEM(coupling.shape, BF16),
            SMEM((slots, leaves), jnp.int32),
            SMEM((slots, leaves), jnp.int32),
            VMEM((leaves + inner, size, 2 * size), F32),
            VMEM((leaves + inner, size, 2 * size), F32),
            VMEM((2 * leaves, size, size), BF16),
            VMEM((leaves, slots, size, size), BF16),
            VMEM((n_send, size // 2, 2 * size), F32),
            VMEM((n_recv, size // 2, 2 * size), F32),
            VMEM((blocks - 1, leaves // blocks, size, size), BF16),
            VMEM((blocks - 1, leaves // blocks, size, size), BF16),
            pltpu.SemaphoreType.DMA((8,)),
            pltpu.SemaphoreType.DMA((5,)),
            pltpu.SemaphoreType.DMA((n_recv,)),
            pltpu.SemaphoreType.DMA((n_recv,)),
            pltpu.SemaphoreType.DMA((2,)),
            pltpu.SemaphoreType.DMA((2,)),
            pltpu.SemaphoreType.DMA((blocks - 1,)),
            pltpu.SemaphoreType.DMA((blocks - 1,)),
        ],
        compiler_params=pltpu.CompilerParams(
            collective_id=0, has_side_effects=True, vmem_limit_bytes=60 * 2**20
        ),
    )(
        leaf_pairing,
        leaf_basis,
        leaf_transfer,
        inner_transfer[0],
        moves,
        coupling,
        source_cluster_index.T,
        coupling_slot_mask.T,
    )

    upper_factor, q, inner_factor, projected, row_weight = pl.pallas_call(
        last_kernel,
        out_shape=(upper_shape, q_shape, inner_shape, projected_shape, weight_shape),
        in_specs=[vmem] + [anywhere] * 4,
        out_specs=(vmem,) + (anywhere,) * 4,
        scratch_shapes=[
            VMEM((depth, size, 2 * size), F32),
            VMEM((depth, size, 2 * size), F32),
            pltpu.SemaphoreType.DMA((4,)),
        ],
        compiler_params=pltpu.CompilerParams(vmem_limit_bytes=60 * 2**20),
    )(upper_gram, q, inner_factor, projected, row_weight)
    return (q, inner_factor[None], upper_factor[None], projected, row_weight)


def solution(mesh):
    placed = (
        P("leaf", None, None),
        P("leaf", None),
        P("leaf", None, None),
        P("leaf", None, None, None),
        P(),
        P("leaf", "blk", None, None),
        P("leaf", "blk"),
        P("leaf", "blk"),
    )
    return jax.shard_map(
        local,
        mesh=mesh,
        in_specs=placed,
        out_specs=(
            P("leaf", None, "blk"),
            P("leaf", None, None, None),
            P("leaf", None, None, None),
            P("leaf", "blk", None, None),
            P(("leaf", "blk"), None, None),
        ),
        check_vma=False,
    )
```

```python
import functools
import math

import jax
import jax.numpy as jnp
from jax import lax
from jax.experimental import pallas as pl
from jax.experimental.pallas import tpu as pltpu
from jax.sharding import PartitionSpec as P

F32 = jnp.float32
BF16 = jnp.bfloat16
VMEM = pltpu.VMEM
SMEM = pltpu.SMEM


def split(x):
    high = x.astype(BF16)
    return high, (x - high.astype(F32)).astype(BF16)


def dot_nn(a, b):
    return lax.dot_general(a, b, (((1,), (0,)), ((), ())), preferred_element_type=F32)


def dot_nt(a, b):
    return lax.dot_general(a, b, (((1,), (1,)), ((), ())), preferred_element_type=F32)


def dot_tn(a, b):
    return lax.dot_general(a, b, (((0,), (0,)), ((), ())), preferred_element_type=F32)


def carry(move, gram):
    move_h, move_l = move
    gram_h, gram_l = split(gram)
    right = dot_nn(gram_h, move_h) + dot_nn(gram_l, move_h)
    if move_l is not None:
        right = right + dot_nn(gram_h, move_l)
    right_h, right_l = split(right)
    out = dot_tn(move_h, right_h) + dot_tn(move_h, right_l)
    if move_l is not None:
        out = out + dot_tn(move_l, right_h)
    return out


def panel_chain(panel, start):
    count, rows, _ = panel.shape
    sub = lax.broadcasted_iota(jnp.int32, (1, rows, 128), 1)
    scale = jnp.zeros((count, rows, 128), F32)
    for r in range(rows):
        col = jnp.broadcast_to(panel[:, :, start + r : start + r + 1], panel.shape)
        inv = lax.rsqrt(col[:, r : r + 1, :])
        outer = jnp.where(sub > r, col, 0.0) * panel[:, r : r + 1, :]
        panel = panel - outer * (inv * inv)
        scale = jnp.where(sub == r, inv, scale)
    return panel * scale


def panel_ahead(panel, start):
    count, rows, _ = panel.shape
    sub = lax.broadcasted_iota(jnp.int32, (1, rows, 128), 1)
    scale = jnp.zeros((count, rows, 128), F32)
    cols = [
        jnp.broadcast_to(panel[:, :, start + r : start + r + 1], panel.shape) for r in range(rows)
    ]
    for r in range(rows):
        inv = lax.rsqrt(cols[r][:, r : r + 1, :])
        mult = jnp.where(sub > r, cols[r], 0.0) * (inv * inv)
        panel = panel - mult * panel[:, r : r + 1, :]
        for t in range(r + 1, rows):
            cols[t] = cols[t] - mult * cols[t][:, r : r + 1, :]
        scale = jnp.where(sub == r, inv, scale)
    return panel * scale


def factor_panel(work, done, first, count, rows, k, eliminate):
    size = work.shape[1]
    last = first + count
    panel = eliminate(work[first:last, k : k + rows, :], k)
    done[first:last, k : k + rows, :] = panel
    if k + rows < size:
        high, low = split(panel)
        left = jnp.concatenate([high, low, high], axis=1)
        right = jnp.concatenate([high, high, low], axis=1)
        for i in range(count):
            down = dot_tn(left[i], right[i])
            work[first + i, k + rows : size, :] = (
                work[first + i, k + rows : size, :] - down[k + rows : size, :]
            )


def upper_mask(size):
    return lax.broadcasted_iota(jnp.int32, (size, size), 0) <= lax.broadcasted_iota(
        jnp.int32, (size, size), 1
    )


def eye(size):
    return (
        lax.broadcasted_iota(jnp.int32, (size, size), 0)
        == lax.broadcasted_iota(jnp.int32, (size, size), 1)
    ).astype(F32)


def pack(matrix):
    half = matrix.shape[0] // 2
    return jnp.concatenate([matrix[:half], matrix[half:]], axis=1)


def unpack(packed):
    half = packed.shape[1] // 2
    return jnp.concatenate([packed[:, :half], packed[:, half:]], axis=0)


def tree_kernel(
    pairing_hbm,
    basis_hbm,
    leaf_move_hbm,
    inner_move_hbm,
    table_hbm,
    coupling_hbm,
    index_hbm,
    mask_hbm,
    q_hbm,
    inner_hbm,
    gram_hbm,
    projected_hbm,
    weight_hbm,
    q_out,
    inner_out,
    gram_out,
    projected,
    weight_out,
    pairing,
    basis,
    leaf_move,
    inner_move,
    table,
    moves,
    coupling,
    index,
    mask,
    work,
    done,
    extended,
    packed,
    half_ref,
    squares,
    send,
    recv,
    row_send,
    row_recv,
    in_sem,
    out_sem,
    send_sem,
    recv_sem,
    halo_send_sem,
    halo_recv_sem,
    row_send_sem,
    row_recv_sem,
):
    leaves, size, panels = basis.shape
    inner = inner_move.shape[0]
    slots = coupling.shape[1]
    part = q_out.shape[2]
    halo = leaves // 2
    n_leaf, blocks = lax.axis_size("leaf"), lax.axis_size("blk")
    me, blk = lax.axis_index("leaf"), lax.axis_index("blk")
    after, before = lax.rem(me + 1, n_leaf), lax.rem(me + n_leaf - 1, n_leaf)
    depth = gram_out.shape[0]

    loads = []
    for j, (source, target) in enumerate(
        (
            (basis_hbm, basis),
            (pairing_hbm, pairing),
            (leaf_move_hbm, leaf_move),
            (inner_move_hbm, inner_move),
            (table_hbm, table),
            (coupling_hbm, coupling),
            (index_hbm, index),
            (mask_hbm, mask),
        )
    ):
        load = pltpu.make_async_copy(source, target, in_sem.at[j])
        load.start()
        loads.append(load)

    stores = []

    def store_out(source, target):
        store = pltpu.make_async_copy(source, target, out_sem.at[len(stores)])
        store.start()
        stores.append(store)

    def flipped(apart):
        out, bit = me, 1
        while bit <= apart:
            if apart & bit:
                out = out + bit - 2 * bit * lax.rem(out // bit, 2)
            bit *= 2
        return out

    groups = [(1,)] + [(2 << (2 * g), 4 << (2 * g), 6 << (2 * g)) for g in range((depth - 1) // 2)]
    barrier = pltpu.get_barrier_semaphore()
    total = 0
    for group in groups:
        for apart in group:
            pl.semaphore_signal(barrier, 1, device_id={"leaf": flipped(apart)})
            total += 1
    for peer in (after, before):
        pl.semaphore_signal(barrier, 1, device_id={"leaf": peer})
        total += 1
    for d in range(1, blocks):
        pl.semaphore_signal(barrier, 1, device_id={"blk": lax.rem(blk + d, blocks)})
        total += 1

    used = [0, 0]

    def start_exchange(step, terms):
        firsts = []
        for term in terms:
            send[used[0]] = pack(term)
            firsts.append(used[0])
            used[0] += 1
        started = []
        for j, apart in enumerate(groups[step]):
            parts = firsts if j == 0 else firsts[-1:]
            for source in parts:
                at = used[1]
                used[1] += 1
                copy = pltpu.make_async_remote_copy(
                    src_ref=send.at[source],
                    dst_ref=recv.at[at],
                    send_sem=send_sem.at[at],
                    recv_sem=recv_sem.at[at],
                    device_id={"leaf": flipped(apart)},
                )
                copy.start()
                started.append((copy, source, at))
        return started

    def finish_exchange(started):
        sums = {}
        for copy, source, at in started:
            copy.wait_recv()
            sums[source] = sums.get(source, send[source]) + recv[at]
        return [unpack(sums[s]) for s in sorted(sums)]

    grams, going = [], []

    def advance():
        grams.extend(finish_exchange(going[-1]))
        if len(going) < len(groups):
            level = len(grams)
            near = unpack(moves[level - 1]).astype(BF16)
            far = split(dot_nn(near, unpack(moves[level]).astype(BF16)))
            terms = [carry((near, None), grams[-1]), carry(far, grams[-1])]
            going.append(start_exchange(len(going), terms))

    identity = eye(size)
    for i in range(leaves + inner):
        work[i, :, size : 2 * size] = identity
    loads[0].wait()
    for i in range(leaves):
        work[i, :, 0:size] = dot_nt(basis[i], basis[i])
    for j in (1, 2, 3):
        loads[j].wait()
    for m in range(leaves // 2):
        a, b = pairing[0, 2 * m], pairing[0, 2 * m + 1]
        work[leaves + m, :, 0:size] = carry(split(leaf_move[a]), work[a, :, 0:size]) + carry(
            split(leaf_move[b]), work[b, :, 0:size]
        )
    below, count = 0, leaves // 2
    while count > 1:
        for m in range(count // 2):
            a = below + 2 * m
            work[leaves + below + count + m, :, 0:size] = carry(
                split(inner_move[a]), work[leaves + a, :, 0:size]
            ) + carry(split(inner_move[a + 1]), work[leaves + a + 1, :, 0:size])
        below, count = below + count, count // 2
    root = carry(split(inner_move[inner - 1]), work[leaves + inner - 1, :, 0:size])
    pl.semaphore_wait(barrier, total)
    going.append(start_exchange(0, [root]))
    for j in (4, 5, 6, 7):
        loads[j].wait()
    level = lax.broadcasted_iota(jnp.int32, (8, n_leaf), 0)
    column = lax.broadcasted_iota(jnp.int32, (8, n_leaf), 1)
    choose = jnp.zeros((8, n_leaf), F32)
    for j in range(1, depth):
        owner = me // (1 << j) * (1 << j) + (1 << (j - 1))
        choose = jnp.where((level == j - 1) & (column == owner), 1.0, choose)
    choose = choose.astype(BF16)
    for b in range(size // 2):
        both = jnp.concatenate([table[b], table[size // 2 + b]], axis=0)
        moves[:, b, :] = dot_nt(choose, both)[: depth - 1]

    rows = 16
    for k in range(0, size, rows):
        factor_panel(work, done, 0, leaves + inner, rows, k, panel_chain)
        if k + rows < size:
            advance()

    keep = upper_mask(size)
    for i in range(leaves):
        low = jnp.where(keep, done[i, :, 0:size], 0.0)
        extended[halo + i] = low.astype(BF16)
        packed[halo + i] = pack(low).astype(BF16)
    halo_copies = []
    for j, (peer, source, target) in enumerate(((after, leaves, 0), (before, halo, halo + leaves))):
        copy = pltpu.make_async_remote_copy(
            src_ref=packed.at[pl.ds(source, halo)],
            dst_ref=packed.at[pl.ds(target, halo)],
            send_sem=halo_send_sem.at[j],
            recv_sem=halo_recv_sem.at[j],
            device_id={"leaf": peer},
        )
        copy.start()
        halo_copies.append(copy)

    for t in range(leaves):
        for s in range(slots):
            half_ref[t, s] = dot_nn(extended[halo + t], coupling[t, s]).astype(BF16)
    for copy in halo_copies:
        copy.wait_recv()
    for i in range(halo):
        extended[i] = unpack(packed[i])
        extended[halo + leaves + i] = unpack(packed[halo + leaves + i])
    per = leaves // blocks
    base = me * leaves - halo
    row_scale = 1.0 / (slots * blocks * size)
    row_copies = []
    for d in range(1, blocks + 1):
        peer = lax.rem(blk + d, blocks)
        for i in range(per):
            t = peer * per + i
            square = None
            for s in range(slots):
                source = jnp.clip(index[s, t] - base, 0, leaves + 2 * halo - 1)
                full = dot_nt(half_ref[t, s], extended[source])
                value = (full * mask[s, t].astype(F32)).astype(BF16)
                projected[t, s] = value
                term = dot_nt(value, value)
                square = term if square is None else square + term
            squares[d - 1, i] = square * row_scale
        if d < blocks:
            for i in range(per):
                row_send[d - 1, i] = pack(squares[d - 1, i]).astype(BF16)
            copy = pltpu.make_async_remote_copy(
                src_ref=row_send.at[d - 1],
                dst_ref=row_recv.at[d - 1],
                send_sem=row_send_sem.at[d - 1],
                recv_sem=row_recv_sem.at[d - 1],
                device_id={"blk": peer},
            )
            copy.start()
            row_copies.append(copy)
    store_out(projected, projected_hbm)
    begin = pl.multiple_of(blk * part, part)
    for i in range(leaves):
        weights = (math.sqrt(panels) * done[i, :, size : 2 * size]).astype(BF16)
        q_out[i] = dot_nn(weights, basis[i, :, pl.ds(begin, part)]).astype(BF16)
    for i in range(inner):
        inner_out[i] = jnp.where(keep, done[leaves + i, :, 0:size], 0.0)
    store_out(q_out, q_hbm)
    store_out(inner_out, inner_hbm)
    advance()
    for i in range(depth):
        gram_out[i] = grams[i]
    store_out(gram_out, gram_hbm)
    for copy in row_copies:
        copy.wait_recv()
    for i in range(per):
        square = row_recv[0, i].astype(F32)
        for d in range(1, blocks - 1):
            square = square + row_recv[d, i].astype(F32)
        weight_out[i] = squares[blocks - 1, i] + unpack(square)
    store_out(weight_out, weight_hbm)
    for started in going:
        for copy, _, _ in started:
            copy.wait_send()
    for copy in halo_copies + row_copies:
        copy.wait_send()
    for store in stores:
        store.wait()


def last_kernel(
    gram_hbm,
    q,
    inner,
    projected,
    weight,
    upper_out,
    q_out,
    inner_out,
    projected_out,
    weight_out,
    gram,
    q_held,
    inner_held,
    projected_held,
    weight_held,
    work,
    done,
    gram_sem,
    in_sem,
    out_sem,
):
    depth, size, _ = gram.shape
    first = pltpu.make_async_copy(gram_hbm, gram, gram_sem)
    first.start()
    loads, stores = [], []
    for j, (source, held, target) in enumerate(
        (
            (projected, projected_held, projected_out),
            (q, q_held, q_out),
            (inner, inner_held, inner_out),
            (weight, weight_held, weight_out),
        )
    ):
        loads.append(pltpu.make_async_copy(source, held, in_sem.at[j]))
        stores.append(pltpu.make_async_copy(held, target, out_sem.at[j]))
        loads[-1].start()
    first.wait()
    for i in range(depth):
        work[i, :, 0:size] = gram[i]
        work[i, :, size : 2 * size] = jnp.zeros((size, size), F32)
    rows = 8
    for k in range(0, size, rows):
        factor_panel(work, done, 0, depth, rows, k, panel_ahead)
        if k == 3 * rows:
            for load, store in zip(loads, stores):
                load.wait()
                store.start()
    keep = upper_mask(size)
    for i in range(depth):
        upper_out[i] = jnp.where(keep, done[i, :, 0:size], 0.0)
    for store in stores:
        store.wait()


def local(
    leaf_basis,
    leaf_pairing,
    leaf_transfer,
    inner_transfer,
    upper_transfer,
    coupling,
    source_cluster_index,
    coupling_slot_mask,
):
    leaves, size, panels = leaf_basis.shape
    inner = inner_transfer.shape[1]
    n_leaf, blocks = lax.axis_size("leaf"), lax.axis_size("blk")
    depth = n_leaf.bit_length() - 1
    slots = coupling.shape[1]
    part = panels // blocks
    vmem = pl.BlockSpec(memory_space=VMEM)
    anywhere = pl.BlockSpec(memory_space=pl.ANY)

    n_recv = 1 + 4 * ((depth - 1) // 2)
    n_send = 1 + 2 * ((depth - 1) // 2)
    q_shape = jax.ShapeDtypeStruct((leaves, size, part), BF16)
    inner_shape = jax.ShapeDtypeStruct((inner, size, size), F32)
    upper_shape = jax.ShapeDtypeStruct((depth, size, size), F32)
    projected_shape = jax.ShapeDtypeStruct(coupling.shape, BF16)
    weight_shape = jax.ShapeDtypeStruct((leaves // blocks, size, size), F32)
    q, inner_factor, upper_gram, projected, row_weight = pl.pallas_call(
        tree_kernel,
        out_shape=(q_shape, inner_shape, upper_shape, projected_shape, weight_shape),
        in_specs=[anywhere] * 8,
        out_specs=(anywhere,) * 5,
        scratch_shapes=[
            VMEM(q_shape.shape, BF16),
            VMEM(inner_shape.shape, F32),
            VMEM(upper_shape.shape, F32),
            VMEM(coupling.shape, BF16),
            VMEM(weight_shape.shape, F32),
            SMEM((1, leaves), jnp.int32),
            VMEM((leaves, size, panels), BF16),
            VMEM((leaves, size, size), F32),
            VMEM((inner, size, size), F32),
            VMEM((size, size, n_leaf), BF16),
            VMEM((depth - 1, size // 2, 2 * size), F32),
            VMEM(coupling.shape, BF16),
            SMEM((slots, leaves), jnp.int32),
            SMEM((slots, leaves), jnp.int32),
            VMEM((leaves + inner, size, 2 * size), F32),
            VMEM((leaves + inner, size, 2 * size), F32),
            VMEM((2 * leaves, size, size), BF16),
            VMEM((2 * leaves, size // 2, 2 * size), BF16),
            VMEM((leaves, slots, size, size), BF16),
            VMEM((blocks, leaves // blocks, size, size), F32),
            VMEM((n_send, size // 2, 2 * size), F32),
            VMEM((n_recv, size // 2, 2 * size), F32),
            VMEM((blocks - 1, leaves // blocks, size // 2, 2 * size), BF16),
            VMEM((blocks - 1, leaves // blocks, size // 2, 2 * size), BF16),
            pltpu.SemaphoreType.DMA((8,)),
            pltpu.SemaphoreType.DMA((5,)),
            pltpu.SemaphoreType.DMA((n_recv,)),
            pltpu.SemaphoreType.DMA((n_recv,)),
            pltpu.SemaphoreType.DMA((2,)),
            pltpu.SemaphoreType.DMA((2,)),
            pltpu.SemaphoreType.DMA((blocks - 1,)),
            pltpu.SemaphoreType.DMA((blocks - 1,)),
        ],
        compiler_params=pltpu.CompilerParams(
            collective_id=0, has_side_effects=True, vmem_limit_bytes=60 * 2**20
        ),
    )(
        leaf_pairing,
        leaf_basis,
        leaf_transfer,
        inner_transfer[0],
        jnp.transpose(upper_transfer, (1, 2, 0)),
        coupling,
        source_cluster_index.T,
        coupling_slot_mask.T,
    )

    upper_factor, q, inner_factor, projected, row_weight = pl.pallas_call(
        last_kernel,
        out_shape=(upper_shape, q_shape, inner_shape, projected_shape, weight_shape),
        in_specs=[anywhere] * 5,
        out_specs=(vmem,) + (anywhere,) * 4,
        scratch_shapes=[
            VMEM(upper_shape.shape, F32),
            VMEM(q_shape.shape, BF16),
            VMEM(inner_shape.shape, F32),
            VMEM(coupling.shape, BF16),
            VMEM(weight_shape.shape, F32),
            VMEM((depth, size, 2 * size), F32),
            VMEM((depth, size, 2 * size), F32),
            pltpu.SemaphoreType.DMA,
            pltpu.SemaphoreType.DMA((4,)),
            pltpu.SemaphoreType.DMA((4,)),
        ],
        compiler_params=pltpu.CompilerParams(vmem_limit_bytes=60 * 2**20),
    )(upper_gram, q, inner_factor, projected, row_weight)
    return (q, inner_factor[None], upper_factor[None], projected, row_weight)


def solution(mesh):
    placed = (
        P("leaf", None, None),
        P("leaf", None),
        P("leaf", None, None),
        P("leaf", None, None, None),
        P(),
        P("leaf", "blk", None, None),
        P("leaf", "blk"),
        P("leaf", "blk"),
    )
    return jax.shard_map(
        local,
        mesh=mesh,
        in_specs=placed,
        out_specs=(
            P("leaf", None, "blk"),
            P("leaf", None, None, None),
            P("leaf", None, None, None),
            P("leaf", "blk", None, None),
            P(("leaf", "blk"), None, None),
        ),
        check_vma=False,
    )
```

```python
import functools
import math

import jax
import jax.numpy as jnp
from jax import lax
from jax.experimental import pallas as pl
from jax.experimental.pallas import tpu as pltpu
from jax.sharding import PartitionSpec as P

F32 = jnp.float32
BF16 = jnp.bfloat16
VMEM = pltpu.VMEM
SMEM = pltpu.SMEM


def split(x):
    high = x.astype(BF16)
    return high, (x - high.astype(F32)).astype(BF16)


def dot_nn(a, b):
    return lax.dot_general(a, b, (((1,), (0,)), ((), ())), preferred_element_type=F32)


def dot_nt(a, b):
    return lax.dot_general(a, b, (((1,), (1,)), ((), ())), preferred_element_type=F32)


def dot_tn(a, b):
    return lax.dot_general(a, b, (((0,), (0,)), ((), ())), preferred_element_type=F32)


def carry(move, gram):
    move_h, move_l = move
    gram_h, gram_l = split(gram)
    right = dot_nn(gram_h, move_h) + dot_nn(gram_l, move_h)
    if move_l is not None:
        right = right + dot_nn(gram_h, move_l)
    right_h, right_l = split(right)
    out = dot_tn(move_h, right_h) + dot_tn(move_h, right_l)
    if move_l is not None:
        out = out + dot_tn(move_l, right_h)
    return out


def panel_chain(panel, start):
    count, rows, _ = panel.shape
    sub = lax.broadcasted_iota(jnp.int32, (1, rows, 128), 1)
    scale = jnp.zeros((count, rows, 128), F32)
    for r in range(rows):
        col = jnp.broadcast_to(panel[:, :, start + r : start + r + 1], panel.shape)
        inv = lax.rsqrt(col[:, r : r + 1, :])
        outer = jnp.where(sub > r, col, 0.0) * panel[:, r : r + 1, :]
        panel = panel - outer * (inv * inv)
        scale = jnp.where(sub == r, inv, scale)
    return panel * scale


def panel_ahead(panel, start):
    count, rows, _ = panel.shape
    sub = lax.broadcasted_iota(jnp.int32, (1, rows, 128), 1)
    scale = jnp.zeros((count, rows, 128), F32)
    cols = [
        jnp.broadcast_to(panel[:, :, start + r : start + r + 1], panel.shape) for r in range(rows)
    ]
    for r in range(rows):
        inv = lax.rsqrt(cols[r][:, r : r + 1, :])
        mult = jnp.where(sub > r, cols[r], 0.0) * (inv * inv)
        panel = panel - mult * panel[:, r : r + 1, :]
        for t in range(r + 1, rows):
            cols[t] = cols[t] - mult * cols[t][:, r : r + 1, :]
        scale = jnp.where(sub == r, inv, scale)
    return panel * scale


def factor_panel(work, done, first, count, rows, k, eliminate):
    size = work.shape[1]
    last = first + count
    panel = eliminate(work[first:last, k : k + rows, :], k)
    done[first:last, k : k + rows, :] = panel
    if k + rows < size:
        high, low = split(panel)
        left = jnp.concatenate([high, low, high], axis=1)
        right = jnp.concatenate([high, high, low], axis=1)
        for i in range(count):
            down = dot_tn(left[i], right[i])
            work[first + i, k + rows : size, :] = (
                work[first + i, k + rows : size, :] - down[k + rows : size, :]
            )


def upper_mask(size):
    return lax.broadcasted_iota(jnp.int32, (size, size), 0) <= lax.broadcasted_iota(
        jnp.int32, (size, size), 1
    )


def eye(size):
    return (
        lax.broadcasted_iota(jnp.int32, (size, size), 0)
        == lax.broadcasted_iota(jnp.int32, (size, size), 1)
    ).astype(F32)


def pack(matrix):
    half = matrix.shape[0] // 2
    return jnp.concatenate([matrix[:half], matrix[half:]], axis=1)


def unpack(packed):
    half = packed.shape[1] // 2
    return jnp.concatenate([packed[:, :half], packed[:, half:]], axis=0)


def tree_kernel(
    pairing_hbm,
    basis_hbm,
    leaf_move_hbm,
    inner_move_hbm,
    table_hbm,
    coupling_hbm,
    index_hbm,
    mask_hbm,
    q_hbm,
    inner_hbm,
    gram_hbm,
    projected_hbm,
    weight_hbm,
    q_out,
    inner_out,
    gram_out,
    projected,
    weight_out,
    pairing,
    basis,
    leaf_move,
    inner_move,
    table,
    moves,
    coupling,
    index,
    mask,
    work,
    done,
    extended,
    packed,
    half_ref,
    squares,
    send,
    recv,
    row_send,
    row_recv,
    in_sem,
    out_sem,
    send_sem,
    recv_sem,
    halo_send_sem,
    halo_recv_sem,
    row_send_sem,
    row_recv_sem,
):
    leaves, size, panels = basis.shape
    inner = inner_move.shape[0]
    slots = coupling.shape[1]
    part = q_out.shape[2]
    halo = leaves // 2
    n_leaf, blocks = lax.axis_size("leaf"), lax.axis_size("blk")
    me, blk = lax.axis_index("leaf"), lax.axis_index("blk")
    after, before = lax.rem(me + 1, n_leaf), lax.rem(me + n_leaf - 1, n_leaf)
    depth = gram_out.shape[0]

    loads = []
    for j, (source, target) in enumerate(
        (
            (basis_hbm, basis),
            (pairing_hbm, pairing),
            (leaf_move_hbm, leaf_move),
            (inner_move_hbm, inner_move),
            (table_hbm, table),
            (coupling_hbm, coupling),
            (index_hbm, index),
            (mask_hbm, mask),
        )
    ):
        load = pltpu.make_async_copy(source, target, in_sem.at[j])
        load.start()
        loads.append(load)

    stores = []

    def store_out(source, target):
        store = pltpu.make_async_copy(source, target, out_sem.at[len(stores)])
        store.start()
        stores.append(store)

    def flipped(apart):
        out, bit = me, 1
        while bit <= apart:
            if apart & bit:
                out = out + bit - 2 * bit * lax.rem(out // bit, 2)
            bit *= 2
        return out

    groups = [(1,)] + [(2 << (2 * g), 4 << (2 * g), 6 << (2 * g)) for g in range((depth - 1) // 2)]
    barrier = pltpu.get_barrier_semaphore()
    total = 0
    for group in groups:
        for apart in group:
            pl.semaphore_signal(barrier, 1, device_id={"leaf": flipped(apart)})
            total += 1
    for peer in (after, before):
        pl.semaphore_signal(barrier, 1, device_id={"leaf": peer})
        total += 1
    for d in range(1, blocks):
        pl.semaphore_signal(barrier, 1, device_id={"blk": lax.rem(blk + d, blocks)})
        total += 1

    used = [0, 0]

    def start_exchange(step, terms):
        firsts = []
        for term in terms:
            send[used[0]] = pack(term)
            firsts.append(used[0])
            used[0] += 1
        started = []
        for j, apart in enumerate(groups[step]):
            parts = firsts if j == 0 else firsts[-1:]
            for source in parts:
                at = used[1]
                used[1] += 1
                copy = pltpu.make_async_remote_copy(
                    src_ref=send.at[source],
                    dst_ref=recv.at[at],
                    send_sem=send_sem.at[at],
                    recv_sem=recv_sem.at[at],
                    device_id={"leaf": flipped(apart)},
                )
                copy.start()
                started.append((copy, source, at))
        return started

    def finish_exchange(started):
        sums = {}
        for copy, source, at in started:
            copy.wait_recv()
            sums[source] = sums.get(source, send[source]) + recv[at]
        return [unpack(sums[s]) for s in sorted(sums)]

    grams, going = [], []

    def advance():
        grams.extend(finish_exchange(going[-1]))
        if len(going) < len(groups):
            level = len(grams)
            near = unpack(moves[level - 1]).astype(BF16)
            far = split(dot_nn(near, unpack(moves[level]).astype(BF16)))
            terms = [carry((near, None), grams[-1]), carry(far, grams[-1])]
            going.append(start_exchange(len(going), terms))

    identity = eye(size)
    for i in range(leaves + inner):
        work[i, :, size : 2 * size] = identity
    loads[0].wait()
    for i in range(leaves):
        work[i, :, 0:size] = dot_nt(basis[i], basis[i])
    for j in (1, 2, 3):
        loads[j].wait()
    for m in range(leaves // 2):
        a, b = pairing[0, 2 * m], pairing[0, 2 * m + 1]
        work[leaves + m, :, 0:size] = carry(split(leaf_move[a]), work[a, :, 0:size]) + carry(
            split(leaf_move[b]), work[b, :, 0:size]
        )
    below, count = 0, leaves // 2
    while count > 1:
        for m in range(count // 2):
            a = below + 2 * m
            work[leaves + below + count + m, :, 0:size] = carry(
                split(inner_move[a]), work[leaves + a, :, 0:size]
            ) + carry(split(inner_move[a + 1]), work[leaves + a + 1, :, 0:size])
        below, count = below + count, count // 2
    root = carry(split(inner_move[inner - 1]), work[leaves + inner - 1, :, 0:size])
    pl.semaphore_wait(barrier, total)
    going.append(start_exchange(0, [root]))
    for j in (4, 5, 6, 7):
        loads[j].wait()
    level = lax.broadcasted_iota(jnp.int32, (8, n_leaf), 0)
    column = lax.broadcasted_iota(jnp.int32, (8, n_leaf), 1)
    choose = jnp.zeros((8, n_leaf), F32)
    for j in range(1, depth):
        owner = me // (1 << j) * (1 << j) + (1 << (j - 1))
        choose = jnp.where((level == j - 1) & (column == owner), 1.0, choose)
    choose = choose.astype(BF16)
    for b in range(size // 2):
        both = jnp.concatenate([table[b], table[size // 2 + b]], axis=0)
        moves[:, b, :] = dot_nt(choose, both)[: depth - 1]

    rows = 16
    for k in range(0, size, rows):
        factor_panel(work, done, 0, leaves + inner, rows, k, panel_chain)
        if k % (2 * rows) == rows:
            advance()

    keep = upper_mask(size)
    for i in range(leaves):
        low = jnp.where(keep, done[i, :, 0:size], 0.0)
        extended[halo + i] = low.astype(BF16)
        packed[halo + i] = pack(low).astype(BF16)
    halo_copies = []
    for j, (peer, source, target) in enumerate(((after, leaves, 0), (before, halo, halo + leaves))):
        copy = pltpu.make_async_remote_copy(
            src_ref=packed.at[pl.ds(source, halo)],
            dst_ref=packed.at[pl.ds(target, halo)],
            send_sem=halo_send_sem.at[j],
            recv_sem=halo_recv_sem.at[j],
            device_id={"leaf": peer},
        )
        copy.start()
        halo_copies.append(copy)

    for t in range(leaves):
        for s in range(slots):
            half_ref[t, s] = dot_nn(extended[halo + t], coupling[t, s]).astype(BF16)
    begin = pl.multiple_of(blk * part, part)
    for i in range(leaves):
        weights = (math.sqrt(panels) * done[i, :, size : 2 * size]).astype(BF16)
        q_out[i] = dot_nn(weights, basis[i, :, pl.ds(begin, part)]).astype(BF16)
    for i in range(inner):
        inner_out[i] = jnp.where(keep, done[leaves + i, :, 0:size], 0.0)
    store_out(q_out, q_hbm)
    store_out(inner_out, inner_hbm)

    for copy in halo_copies:
        copy.wait_recv()
    for i in range(halo):
        extended[i] = unpack(packed[i])
        extended[halo + leaves + i] = unpack(packed[halo + leaves + i])
    per = leaves // blocks
    base = me * leaves - halo
    row_scale = 1.0 / (slots * blocks * size)
    row_copies = []
    for d in range(1, blocks + 1):
        peer = lax.rem(blk + d, blocks)
        for i in range(per):
            t = peer * per + i
            square = None
            for s in range(slots):
                source = jnp.clip(index[s, t] - base, 0, leaves + 2 * halo - 1)
                full = dot_nt(half_ref[t, s], extended[source])
                value = (full * mask[s, t].astype(F32)).astype(BF16)
                projected[t, s] = value
                term = dot_nt(value, value)
                square = term if square is None else square + term
            squares[d - 1, i] = square * row_scale
        if d < blocks:
            for i in range(per):
                row_send[d - 1, i] = pack(squares[d - 1, i]).astype(BF16)
            copy = pltpu.make_async_remote_copy(
                src_ref=row_send.at[d - 1],
                dst_ref=row_recv.at[d - 1],
                send_sem=row_send_sem.at[d - 1],
                recv_sem=row_recv_sem.at[d - 1],
                device_id={"blk": peer},
            )
            copy.start()
            row_copies.append(copy)
    store_out(projected, projected_hbm)
    advance()
    early = len(grams)
    for i in range(early):
        work[i, :, 0:size] = grams[i]
        work[i, :, size : 2 * size] = jnp.zeros((size, size), F32)
    rows = 8
    for k in range(0, size, rows):
        factor_panel(work, done, 0, early, rows, k, panel_ahead)
    for i in range(early):
        gram_out[i] = jnp.where(keep, done[i, :, 0:size], 0.0)
    advance()
    for i in range(early, depth):
        gram_out[i] = grams[i]
    store_out(gram_out, gram_hbm)
    for copy in row_copies:
        copy.wait_recv()
    for i in range(per):
        square = row_recv[0, i].astype(F32)
        for d in range(1, blocks - 1):
            square = square + row_recv[d, i].astype(F32)
        weight_out[i] = squares[blocks - 1, i] + unpack(square)
    store_out(weight_out, weight_hbm)
    for started in going:
        for copy, _, _ in started:
            copy.wait_send()
    for copy in halo_copies + row_copies:
        copy.wait_send()
    for store in stores:
        store.wait()


def last_kernel(
    gram_hbm,
    q,
    inner,
    projected,
    weight,
    upper_out,
    q_out,
    inner_out,
    projected_out,
    weight_out,
    gram,
    q_held,
    inner_held,
    projected_held,
    weight_held,
    work,
    done,
    gram_sem,
    in_sem,
    out_sem,
):
    depth, size, _ = gram.shape
    first = pltpu.make_async_copy(gram_hbm, gram, gram_sem)
    first.start()
    loads, stores = [], []
    for j, (source, held, target) in enumerate(
        (
            (projected, projected_held, projected_out),
            (q, q_held, q_out),
            (inner, inner_held, inner_out),
            (weight, weight_held, weight_out),
        )
    ):
        loads.append(pltpu.make_async_copy(source, held, in_sem.at[j]))
        stores.append(pltpu.make_async_copy(held, target, out_sem.at[j]))
        loads[-1].start()
    first.wait()
    late = work.shape[0]
    for i in range(depth - late):
        upper_out[i] = gram[i]
    for i in range(late):
        work[i, :, 0:size] = gram[depth - late + i]
        work[i, :, size : 2 * size] = jnp.zeros((size, size), F32)
    rows = 16
    for k in range(0, size, rows):
        factor_panel(work, done, 0, late, rows, k, panel_ahead)
        if k == rows:
            for load, store in zip(loads, stores):
                load.wait()
                store.start()
    keep = upper_mask(size)
    for i in range(late):
        upper_out[depth - late + i] = jnp.where(keep, done[i, :, 0:size], 0.0)
    for store in stores:
        store.wait()


def local(
    leaf_basis,
    leaf_pairing,
    leaf_transfer,
    inner_transfer,
    upper_transfer,
    coupling,
    source_cluster_index,
    coupling_slot_mask,
):
    leaves, size, panels = leaf_basis.shape
    inner = inner_transfer.shape[1]
    n_leaf, blocks = lax.axis_size("leaf"), lax.axis_size("blk")
    depth = n_leaf.bit_length() - 1
    slots = coupling.shape[1]
    part = panels // blocks
    vmem = pl.BlockSpec(memory_space=VMEM)
    anywhere = pl.BlockSpec(memory_space=pl.ANY)

    n_recv = 1 + 4 * ((depth - 1) // 2)
    n_send = 1 + 2 * ((depth - 1) // 2)
    q_shape = jax.ShapeDtypeStruct((leaves, size, part), BF16)
    inner_shape = jax.ShapeDtypeStruct((inner, size, size), F32)
    upper_shape = jax.ShapeDtypeStruct((depth, size, size), F32)
    projected_shape = jax.ShapeDtypeStruct(coupling.shape, BF16)
    weight_shape = jax.ShapeDtypeStruct((leaves // blocks, size, size), F32)
    q, inner_factor, upper_gram, projected, row_weight = pl.pallas_call(
        tree_kernel,
        out_shape=(q_shape, inner_shape, upper_shape, projected_shape, weight_shape),
        in_specs=[anywhere] * 8,
        out_specs=(anywhere,) * 5,
        scratch_shapes=[
            VMEM(q_shape.shape, BF16),
            VMEM(inner_shape.shape, F32),
            VMEM(upper_shape.shape, F32),
            VMEM(coupling.shape, BF16),
            VMEM(weight_shape.shape, F32),
            SMEM((1, leaves), jnp.int32),
            VMEM((leaves, size, panels), BF16),
            VMEM((leaves, size, size), F32),
            VMEM((inner, size, size), F32),
            VMEM((size, size, n_leaf), BF16),
            VMEM((depth - 1, size // 2, 2 * size), F32),
            VMEM(coupling.shape, BF16),
            SMEM((slots, leaves), jnp.int32),
            SMEM((slots, leaves), jnp.int32),
            VMEM((leaves + inner, size, 2 * size), F32),
            VMEM((leaves + inner, size, 2 * size), F32),
            VMEM((2 * leaves, size, size), BF16),
            VMEM((2 * leaves, size // 2, 2 * size), BF16),
            VMEM((leaves, slots, size, size), BF16),
            VMEM((blocks, leaves // blocks, size, size), F32),
            VMEM((n_send, size // 2, 2 * size), F32),
            VMEM((n_recv, size // 2, 2 * size), F32),
            VMEM((blocks - 1, leaves // blocks, size // 2, 2 * size), BF16),
            VMEM((blocks - 1, leaves // blocks, size // 2, 2 * size), BF16),
            pltpu.SemaphoreType.DMA((8,)),
            pltpu.SemaphoreType.DMA((5,)),
            pltpu.SemaphoreType.DMA((n_recv,)),
            pltpu.SemaphoreType.DMA((n_recv,)),
            pltpu.SemaphoreType.DMA((2,)),
            pltpu.SemaphoreType.DMA((2,)),
            pltpu.SemaphoreType.DMA((blocks - 1,)),
            pltpu.SemaphoreType.DMA((blocks - 1,)),
        ],
        compiler_params=pltpu.CompilerParams(
            collective_id=0, has_side_effects=True, vmem_limit_bytes=60 * 2**20
        ),
    )(
        leaf_pairing,
        leaf_basis,
        leaf_transfer,
        inner_transfer[0],
        jnp.transpose(upper_transfer, (1, 2, 0)),
        coupling,
        source_cluster_index.T,
        coupling_slot_mask.T,
    )

    upper_factor, q, inner_factor, projected, row_weight = pl.pallas_call(
        last_kernel,
        out_shape=(upper_shape, q_shape, inner_shape, projected_shape, weight_shape),
        in_specs=[anywhere] * 5,
        out_specs=(vmem,) + (anywhere,) * 4,
        scratch_shapes=[
            VMEM(upper_shape.shape, F32),
            VMEM(q_shape.shape, BF16),
            VMEM(inner_shape.shape, F32),
            VMEM(coupling.shape, BF16),
            VMEM(weight_shape.shape, F32),
            VMEM((2, size, 2 * size), F32),
            VMEM((2, size, 2 * size), F32),
            pltpu.SemaphoreType.DMA,
            pltpu.SemaphoreType.DMA((4,)),
            pltpu.SemaphoreType.DMA((4,)),
        ],
        compiler_params=pltpu.CompilerParams(vmem_limit_bytes=60 * 2**20),
    )(upper_gram, q, inner_factor, projected, row_weight)
    return (q, inner_factor[None], upper_factor[None], projected, row_weight)


def solution(mesh):
    placed = (
        P("leaf", None, None),
        P("leaf", None),
        P("leaf", None, None),
        P("leaf", None, None, None),
        P(),
        P("leaf", "blk", None, None),
        P("leaf", "blk"),
        P("leaf", "blk"),
    )
    return jax.shard_map(
        local,
        mesh=mesh,
        in_specs=placed,
        out_specs=(
            P("leaf", None, "blk"),
            P("leaf", None, None, None),
            P("leaf", None, None, None),
            P("leaf", "blk", None, None),
            P(("leaf", "blk"), None, None),
        ),
        check_vma=False,
    )
```

```python
import functools
import math

import jax
import jax.numpy as jnp
from jax import lax
from jax.experimental import pallas as pl
from jax.experimental.pallas import tpu as pltpu
from jax.sharding import PartitionSpec as P

F32 = jnp.float32
BF16 = jnp.bfloat16
VMEM = pltpu.VMEM
SMEM = pltpu.SMEM


def split(x):
    high = x.astype(BF16)
    return high, (x - high.astype(F32)).astype(BF16)


def dot_nn(a, b):
    return lax.dot_general(a, b, (((1,), (0,)), ((), ())), preferred_element_type=F32)


def dot_nt(a, b):
    return lax.dot_general(a, b, (((1,), (1,)), ((), ())), preferred_element_type=F32)


def dot_tn(a, b):
    return lax.dot_general(a, b, (((0,), (0,)), ((), ())), preferred_element_type=F32)


def carry(move, gram):
    move_h, move_l = move
    gram_h, gram_l = split(gram)
    right = dot_nn(gram_h, move_h) + dot_nn(gram_l, move_h)
    if move_l is not None:
        right = right + dot_nn(gram_h, move_l)
    right_h, right_l = split(right)
    out = dot_tn(move_h, right_h) + dot_tn(move_h, right_l)
    if move_l is not None:
        out = out + dot_tn(move_l, right_h)
    return out


def panel_chain(panel, start):
    count, rows, _ = panel.shape
    sub = lax.broadcasted_iota(jnp.int32, (1, rows, 128), 1)
    scale = jnp.zeros((count, rows, 128), F32)
    for r in range(rows):
        col = jnp.broadcast_to(panel[:, :, start + r : start + r + 1], panel.shape)
        inv = lax.rsqrt(col[:, r : r + 1, :])
        outer = jnp.where(sub > r, col, 0.0) * panel[:, r : r + 1, :]
        panel = panel - outer * (inv * inv)
        scale = jnp.where(sub == r, inv, scale)
    return panel * scale


def panel_ahead(panel, start):
    count, rows, _ = panel.shape
    sub = lax.broadcasted_iota(jnp.int32, (1, rows, 128), 1)
    scale = jnp.zeros((count, rows, 128), F32)
    cols = [
        jnp.broadcast_to(panel[:, :, start + r : start + r + 1], panel.shape) for r in range(rows)
    ]
    for r in range(rows):
        inv = lax.rsqrt(cols[r][:, r : r + 1, :])
        mult = jnp.where(sub > r, cols[r], 0.0) * (inv * inv)
        panel = panel - mult * panel[:, r : r + 1, :]
        for t in range(r + 1, rows):
            cols[t] = cols[t] - mult * cols[t][:, r : r + 1, :]
        scale = jnp.where(sub == r, inv, scale)
    return panel * scale


def factor_panel(work, done, first, count, rows, k, eliminate):
    size = work.shape[1]
    last = first + count
    panel = eliminate(work[first:last, k : k + rows, :], k)
    done[first:last, k : k + rows, :] = panel
    if k + rows < size:
        high, low = split(panel)
        left = jnp.concatenate([high, low, high], axis=1)
        right = jnp.concatenate([high, high, low], axis=1)
        for i in range(count):
            down = dot_tn(left[i], right[i])
            work[first + i, k + rows : size, :] = (
                work[first + i, k + rows : size, :] - down[k + rows : size, :]
            )


def upper_mask(size):
    return lax.broadcasted_iota(jnp.int32, (size, size), 0) <= lax.broadcasted_iota(
        jnp.int32, (size, size), 1
    )


def eye(size):
    return (
        lax.broadcasted_iota(jnp.int32, (size, size), 0)
        == lax.broadcasted_iota(jnp.int32, (size, size), 1)
    ).astype(F32)


def pack(matrix):
    half = matrix.shape[0] // 2
    return jnp.concatenate([matrix[:half], matrix[half:]], axis=1)


def unpack(packed):
    half = packed.shape[1] // 2
    return jnp.concatenate([packed[:, :half], packed[:, half:]], axis=0)


def tree_kernel(
    pairing_hbm,
    basis_hbm,
    leaf_move_hbm,
    inner_move_hbm,
    table_hbm,
    coupling_hbm,
    index_hbm,
    mask_hbm,
    q_hbm,
    inner_hbm,
    upper_hbm,
    projected_hbm,
    weight_hbm,
    q_out,
    inner_out,
    upper_out,
    projected,
    weight_out,
    pairing,
    basis,
    leaf_move,
    inner_move,
    table,
    moves,
    path,
    coupling,
    index,
    mask,
    work,
    done,
    extended,
    packed,
    half_ref,
    squares,
    send,
    recv,
    row_send,
    row_recv,
    in_sem,
    out_sem,
    send_sem,
    recv_sem,
    halo_send_sem,
    halo_recv_sem,
    row_send_sem,
    row_recv_sem,
):
    leaves, size, panels = basis.shape
    inner = inner_move.shape[0]
    slots = coupling.shape[1]
    part = q_out.shape[2]
    halo = leaves // 2
    n_leaf, blocks = lax.axis_size("leaf"), lax.axis_size("blk")
    me, blk = lax.axis_index("leaf"), lax.axis_index("blk")
    after, before = lax.rem(me + 1, n_leaf), lax.rem(me + n_leaf - 1, n_leaf)
    depth = upper_out.shape[0]

    loads = []
    for j, (source, target) in enumerate(
        (
            (basis_hbm, basis),
            (pairing_hbm, pairing),
            (leaf_move_hbm, leaf_move),
            (inner_move_hbm, inner_move),
            (table_hbm, table),
            (coupling_hbm, coupling),
            (index_hbm, index),
            (mask_hbm, mask),
        )
    ):
        load = pltpu.make_async_copy(source, target, in_sem.at[j])
        load.start()
        loads.append(load)

    stores = []

    def store_out(source, target):
        store = pltpu.make_async_copy(source, target, out_sem.at[len(stores)])
        store.start()
        stores.append(store)

    def flipped(apart):
        out, bit = me, 1
        while bit <= apart:
            if apart & bit:
                out = out + bit - 2 * bit * lax.rem(out // bit, 2)
            bit *= 2
        return out

    groups = [(1,)] + [(2 << (2 * g), 4 << (2 * g), 6 << (2 * g)) for g in range((depth - 1) // 2)]
    barrier = pltpu.get_barrier_semaphore()
    total = 0
    for group in groups:
        for apart in group:
            pl.semaphore_signal(barrier, 1, device_id={"leaf": flipped(apart)})
            total += 1
    for peer in (after, before):
        pl.semaphore_signal(barrier, 1, device_id={"leaf": peer})
        total += 1
    for d in range(1, blocks):
        pl.semaphore_signal(barrier, 1, device_id={"blk": lax.rem(blk + d, blocks)})
        total += 1

    used = [0, 0]

    def start_exchange(step, terms):
        firsts = []
        for term in terms:
            send[used[0]] = pack(term)
            firsts.append(used[0])
            used[0] += 1
        started = []
        for j, apart in enumerate(groups[step]):
            parts = firsts if j == 0 else firsts[-1:]
            for source in parts:
                at = used[1]
                used[1] += 1
                copy = pltpu.make_async_remote_copy(
                    src_ref=send.at[source],
                    dst_ref=recv.at[at],
                    send_sem=send_sem.at[at],
                    recv_sem=recv_sem.at[at],
                    device_id={"leaf": flipped(apart)},
                )
                copy.start()
                started.append((copy, source, at))
        return started

    def finish_exchange(started):
        sums = {}
        for copy, source, at in started:
            copy.wait_recv()
            sums[source] = sums.get(source, send[source]) + recv[at]
        return [unpack(sums[s]) for s in sorted(sums)]

    grams, going = [], []

    def advance():
        grams.extend(finish_exchange(going[-1]))
        if len(going) < len(groups):
            at = 3 * (len(going) - 1)
            terms = [
                carry((path[at], None), grams[-1]),
                carry((path[at + 1], path[at + 2]), grams[-1]),
            ]
            going.append(start_exchange(len(going), terms))

    identity = eye(size)
    for i in range(leaves + inner):
        work[i, :, size : 2 * size] = identity
    loads[0].wait()
    for i in range(leaves):
        work[i, :, 0:size] = dot_nt(basis[i], basis[i])
    for j in (1, 2, 3):
        loads[j].wait()
    for m in range(leaves // 2):
        a, b = pairing[0, 2 * m], pairing[0, 2 * m + 1]
        work[leaves + m, :, 0:size] = carry(split(leaf_move[a]), work[a, :, 0:size]) + carry(
            split(leaf_move[b]), work[b, :, 0:size]
        )
    below, count = 0, leaves // 2
    while count > 1:
        for m in range(count // 2):
            a = below + 2 * m
            work[leaves + below + count + m, :, 0:size] = carry(
                split(inner_move[a]), work[leaves + a, :, 0:size]
            ) + carry(split(inner_move[a + 1]), work[leaves + a + 1, :, 0:size])
        below, count = below + count, count // 2
    root = carry(split(inner_move[inner - 1]), work[leaves + inner - 1, :, 0:size])
    pl.semaphore_wait(barrier, total)
    going.append(start_exchange(0, [root]))
    for j in (4, 5, 6, 7):
        loads[j].wait()
    level = lax.broadcasted_iota(jnp.int32, (8, n_leaf), 0)
    column = lax.broadcasted_iota(jnp.int32, (8, n_leaf), 1)
    choose = jnp.zeros((8, n_leaf), F32)
    for j in range(1, depth):
        owner = me // (1 << j) * (1 << j) + (1 << (j - 1))
        choose = jnp.where((level == j - 1) & (column == owner), 1.0, choose)
    choose = choose.astype(BF16)
    for b in range(size // 2):
        both = jnp.concatenate([table[b], table[size // 2 + b]], axis=0)
        moves[:, b, :] = dot_nt(choose, both)[: depth - 1]
    for j in range(len(groups) - 1):
        near = unpack(moves[2 * j]).astype(BF16)
        path[3 * j] = near
        far_h, far_l = split(dot_nn(near, unpack(moves[2 * j + 1]).astype(BF16)))
        path[3 * j + 1] = far_h
        path[3 * j + 2] = far_l

    rows = 16
    for k in range(0, size, rows):
        factor_panel(work, done, 0, leaves + inner, rows, k, panel_chain)
        if k % (2 * rows) == 0:
            advance()

    keep = upper_mask(size)
    for i in range(leaves):
        low = jnp.where(keep, done[i, :, 0:size], 0.0)
        extended[halo + i] = low.astype(BF16)
        packed[halo + i] = pack(low).astype(BF16)
    halo_copies = []
    for j, (peer, source, target) in enumerate(((after, leaves, 0), (before, halo, halo + leaves))):
        copy = pltpu.make_async_remote_copy(
            src_ref=packed.at[pl.ds(source, halo)],
            dst_ref=packed.at[pl.ds(target, halo)],
            send_sem=halo_send_sem.at[j],
            recv_sem=halo_recv_sem.at[j],
            device_id={"leaf": peer},
        )
        copy.start()
        halo_copies.append(copy)

    for t in range(leaves):
        for s in range(slots):
            half_ref[t, s] = dot_nn(extended[halo + t], coupling[t, s]).astype(BF16)
    begin = pl.multiple_of(blk * part, part)
    for i in range(leaves):
        weights = (math.sqrt(panels) * done[i, :, size : 2 * size]).astype(BF16)
        q_out[i] = dot_nn(weights, basis[i, :, pl.ds(begin, part)]).astype(BF16)
    for i in range(inner):
        inner_out[i] = jnp.where(keep, done[leaves + i, :, 0:size], 0.0)
    store_out(q_out, q_hbm)
    store_out(inner_out, inner_hbm)

    advance()
    for copy in halo_copies:
        copy.wait_recv()
    for i in range(halo):
        extended[i] = unpack(packed[i])
        extended[halo + leaves + i] = unpack(packed[halo + leaves + i])
    per = leaves // blocks
    base = me * leaves - halo
    row_scale = 1.0 / (slots * blocks * size)
    row_copies = []
    for d in range(1, blocks + 1):
        peer = lax.rem(blk + d, blocks)
        for i in range(per):
            t = peer * per + i
            square = None
            for s in range(slots):
                source = jnp.clip(index[s, t] - base, 0, leaves + 2 * halo - 1)
                full = dot_nt(half_ref[t, s], extended[source])
                value = (full * mask[s, t].astype(F32)).astype(BF16)
                projected[t, s] = value
                term = dot_nt(value, value)
                square = term if square is None else square + term
            squares[d - 1, i] = square * row_scale
        if d < blocks:
            for i in range(per):
                row_send[d - 1, i] = pack(squares[d - 1, i]).astype(BF16)
            copy = pltpu.make_async_remote_copy(
                src_ref=row_send.at[d - 1],
                dst_ref=row_recv.at[d - 1],
                send_sem=row_send_sem.at[d - 1],
                recv_sem=row_recv_sem.at[d - 1],
                device_id={"blk": peer},
            )
            copy.start()
            row_copies.append(copy)
    store_out(projected, projected_hbm)
    advance()
    for i in range(depth):
        work[i, :, 0:size] = grams[i]
        work[i, :, size : 2 * size] = jnp.zeros((size, size), F32)
    rows = 8
    for k in range(0, size, rows):
        factor_panel(work, done, 0, depth, rows, k, panel_ahead)
    for i in range(depth):
        upper_out[i] = jnp.where(keep, done[i, :, 0:size], 0.0)
    store_out(upper_out, upper_hbm)
    for copy in row_copies:
        copy.wait_recv()
    for i in range(per):
        square = row_recv[0, i].astype(F32)
        for d in range(1, blocks - 1):
            square = square + row_recv[d, i].astype(F32)
        weight_out[i] = squares[blocks - 1, i] + unpack(square)
    store_out(weight_out, weight_hbm)
    for started in going:
        for copy, _, _ in started:
            copy.wait_send()
    for copy in halo_copies + row_copies:
        copy.wait_send()
    for store in stores:
        store.wait()


def last_kernel(*refs):
    count = (len(refs) - 2) // 3
    in_sem, out_sem = refs[3 * count :]
    loads, stores = [], []
    for j in range(count):
        held = refs[2 * count + j]
        loads.append(pltpu.make_async_copy(refs[j], held, in_sem.at[j]))
        stores.append(pltpu.make_async_copy(held, refs[count + j], out_sem.at[j]))
        loads[-1].start()
    for load, store in zip(loads, stores):
        load.wait()
        store.start()
    for store in stores:
        store.wait()


def local(
    leaf_basis,
    leaf_pairing,
    leaf_transfer,
    inner_transfer,
    upper_transfer,
    coupling,
    source_cluster_index,
    coupling_slot_mask,
):
    leaves, size, panels = leaf_basis.shape
    inner = inner_transfer.shape[1]
    n_leaf, blocks = lax.axis_size("leaf"), lax.axis_size("blk")
    depth = n_leaf.bit_length() - 1
    slots = coupling.shape[1]
    part = panels // blocks
    anywhere = pl.BlockSpec(memory_space=pl.ANY)

    n_recv = 1 + 4 * ((depth - 1) // 2)
    n_send = 1 + 2 * ((depth - 1) // 2)
    q_shape = jax.ShapeDtypeStruct((leaves, size, part), BF16)
    inner_shape = jax.ShapeDtypeStruct((inner, size, size), F32)
    upper_shape = jax.ShapeDtypeStruct((depth, size, size), F32)
    projected_shape = jax.ShapeDtypeStruct(coupling.shape, BF16)
    weight_shape = jax.ShapeDtypeStruct((leaves // blocks, size, size), F32)
    shapes = (q_shape, inner_shape, upper_shape, projected_shape, weight_shape)
    results = pl.pallas_call(
        tree_kernel,
        out_shape=shapes,
        in_specs=[anywhere] * 8,
        out_specs=(anywhere,) * 5,
        scratch_shapes=[
            VMEM(q_shape.shape, BF16),
            VMEM(inner_shape.shape, F32),
            VMEM(upper_shape.shape, F32),
            VMEM(coupling.shape, BF16),
            VMEM(weight_shape.shape, F32),
            SMEM((1, leaves), jnp.int32),
            VMEM((leaves, size, panels), BF16),
            VMEM((leaves, size, size), F32),
            VMEM((inner, size, size), F32),
            VMEM((size, size, n_leaf), BF16),
            VMEM((depth - 1, size // 2, 2 * size), F32),
            VMEM((3 * ((depth - 1) // 2), size, size), BF16),
            VMEM(coupling.shape, BF16),
            SMEM((slots, leaves), jnp.int32),
            SMEM((slots, leaves), jnp.int32),
            VMEM((leaves + inner, size, 2 * size), F32),
            VMEM((leaves + inner, size, 2 * size), F32),
            VMEM((2 * leaves, size, size), BF16),
            VMEM((2 * leaves, size // 2, 2 * size), BF16),
            VMEM((leaves, slots, size, size), BF16),
            VMEM((blocks, leaves // blocks, size, size), F32),
            VMEM((n_send, size // 2, 2 * size), F32),
            VMEM((n_recv, size // 2, 2 * size), F32),
            VMEM((blocks - 1, leaves // blocks, size // 2, 2 * size), BF16),
            VMEM((blocks - 1, leaves // blocks, size // 2, 2 * size), BF16),
            pltpu.SemaphoreType.DMA((8,)),
            pltpu.SemaphoreType.DMA((5,)),
            pltpu.SemaphoreType.DMA((n_recv,)),
            pltpu.SemaphoreType.DMA((n_recv,)),
            pltpu.SemaphoreType.DMA((2,)),
            pltpu.SemaphoreType.DMA((2,)),
            pltpu.SemaphoreType.DMA((blocks - 1,)),
            pltpu.SemaphoreType.DMA((blocks - 1,)),
        ],
        compiler_params=pltpu.CompilerParams(
            collective_id=0, has_side_effects=True, vmem_limit_bytes=60 * 2**20
        ),
    )(
        leaf_pairing,
        leaf_basis,
        leaf_transfer,
        inner_transfer[0],
        jnp.transpose(upper_transfer, (1, 2, 0)),
        coupling,
        source_cluster_index.T,
        coupling_slot_mask.T,
    )

    q, inner_factor, upper_factor, projected, row_weight = pl.pallas_call(
        last_kernel,
        out_shape=shapes,
        in_specs=[anywhere] * 5,
        out_specs=(anywhere,) * 5,
        scratch_shapes=[VMEM(shape.shape, shape.dtype) for shape in shapes]
        + [pltpu.SemaphoreType.DMA((5,)), pltpu.SemaphoreType.DMA((5,))],
        compiler_params=pltpu.CompilerParams(vmem_limit_bytes=60 * 2**20),
    )(*results)
    return (q, inner_factor[None], upper_factor[None], projected, row_weight)


def solution(mesh):
    placed = (
        P("leaf", None, None),
        P("leaf", None),
        P("leaf", None, None),
        P("leaf", None, None, None),
        P(),
        P("leaf", "blk", None, None),
        P("leaf", "blk"),
        P("leaf", "blk"),
    )
    return jax.shard_map(
        local,
        mesh=mesh,
        in_specs=placed,
        out_specs=(
            P("leaf", None, "blk"),
            P("leaf", None, None, None),
            P("leaf", None, None, None),
            P("leaf", "blk", None, None),
            P(("leaf", "blk"), None, None),
        ),
        check_vma=False,
    )
```

```python
import functools
import math

import jax
import jax.numpy as jnp
from jax import lax
from jax.experimental import pallas as pl
from jax.experimental.pallas import tpu as pltpu
from jax.sharding import PartitionSpec as P

F32 = jnp.float32
BF16 = jnp.bfloat16
VMEM = pltpu.VMEM
SMEM = pltpu.SMEM
PARTNERS = ((1,), (2, 4, 6), (8,), (24,), (32, 64, 96))


def split(x):
    high = x.astype(BF16)
    return high, (x - high.astype(F32)).astype(BF16)


def dot_nn(a, b):
    return lax.dot_general(a, b, (((1,), (0,)), ((), ())), preferred_element_type=F32)


def dot_nt(a, b):
    return lax.dot_general(a, b, (((1,), (1,)), ((), ())), preferred_element_type=F32)


def dot_tn(a, b):
    return lax.dot_general(a, b, (((0,), (0,)), ((), ())), preferred_element_type=F32)


def carry(move, gram):
    move_h, move_l = move
    gram_h, gram_l = split(gram)
    right = dot_nn(gram_h, move_h) + dot_nn(gram_l, move_h)
    if move_l is not None:
        right = right + dot_nn(gram_h, move_l)
    right_h, right_l = split(right)
    out = dot_tn(move_h, right_h) + dot_tn(move_h, right_l)
    if move_l is not None:
        out = out + dot_tn(move_l, right_h)
    return out


def panel_chain(panel, start):
    count, rows, _ = panel.shape
    sub = lax.broadcasted_iota(jnp.int32, (1, rows, 128), 1)
    scale = jnp.zeros((count, rows, 128), F32)
    for r in range(rows):
        col = jnp.broadcast_to(panel[:, :, start + r : start + r + 1], panel.shape)
        inv = lax.rsqrt(col[:, r : r + 1, :])
        outer = jnp.where(sub > r, col, 0.0) * panel[:, r : r + 1, :]
        panel = panel - outer * (inv * inv)
        scale = jnp.where(sub == r, inv, scale)
    return panel * scale


def panel_ahead(panel, start):
    count, rows, _ = panel.shape
    sub = lax.broadcasted_iota(jnp.int32, (1, rows, 128), 1)
    scale = jnp.zeros((count, rows, 128), F32)
    cols = [
        jnp.broadcast_to(panel[:, :, start + r : start + r + 1], panel.shape) for r in range(rows)
    ]
    for r in range(rows):
        inv = lax.rsqrt(cols[r][:, r : r + 1, :])
        mult = jnp.where(sub > r, cols[r], 0.0) * (inv * inv)
        panel = panel - mult * panel[:, r : r + 1, :]
        for t in range(r + 1, rows):
            cols[t] = cols[t] - mult * cols[t][:, r : r + 1, :]
        scale = jnp.where(sub == r, inv, scale)
    return panel * scale


def factor_panel(work, done, first, count, rows, k, eliminate):
    size = work.shape[1]
    last = first + count
    panel = eliminate(work[first:last, k : k + rows, :], k)
    done[first:last, k : k + rows, :] = panel
    if k + rows < size:
        high, low = split(panel)
        left = jnp.concatenate([high, low, high], axis=1)
        right = jnp.concatenate([high, high, low], axis=1)
        for i in range(count):
            down = dot_tn(left[i], right[i])
            work[first + i, k + rows : size, :] = (
                work[first + i, k + rows : size, :] - down[k + rows : size, :]
            )


def upper_mask(size):
    return lax.broadcasted_iota(jnp.int32, (size, size), 0) <= lax.broadcasted_iota(
        jnp.int32, (size, size), 1
    )


def eye(size):
    return (
        lax.broadcasted_iota(jnp.int32, (size, size), 0)
        == lax.broadcasted_iota(jnp.int32, (size, size), 1)
    ).astype(F32)


def pack(matrix):
    half = matrix.shape[0] // 2
    return jnp.concatenate([matrix[:half], matrix[half:]], axis=1)


def unpack(packed):
    half = packed.shape[1] // 2
    return jnp.concatenate([packed[:, :half], packed[:, half:]], axis=0)


def tree_kernel(
    pairing_hbm,
    basis_hbm,
    leaf_move_hbm,
    inner_move_hbm,
    table_hbm,
    coupling_hbm,
    index_hbm,
    mask_hbm,
    q_hbm,
    inner_hbm,
    upper_hbm,
    projected_hbm,
    weight_hbm,
    q_out,
    inner_out,
    upper_out,
    projected,
    weight_out,
    pairing,
    basis,
    leaf_move,
    inner_move,
    table,
    moves,
    path,
    coupling,
    index,
    mask,
    work,
    done,
    extended,
    packed,
    half_ref,
    squares,
    send,
    recv,
    row_send,
    row_recv,
    in_sem,
    out_sem,
    send_sem,
    recv_sem,
    halo_send_sem,
    halo_recv_sem,
    row_send_sem,
    row_recv_sem,
):
    leaves, size, panels = basis.shape
    inner = inner_move.shape[0]
    slots = coupling.shape[1]
    part = q_out.shape[2]
    halo = leaves // 2
    n_leaf, blocks = lax.axis_size("leaf"), lax.axis_size("blk")
    me, blk = lax.axis_index("leaf"), lax.axis_index("blk")
    after, before = lax.rem(me + 1, n_leaf), lax.rem(me + n_leaf - 1, n_leaf)
    depth = upper_out.shape[0]

    loads = []
    for j, (source, target) in enumerate(
        (
            (basis_hbm, basis),
            (pairing_hbm, pairing),
            (leaf_move_hbm, leaf_move),
            (inner_move_hbm, inner_move),
            (table_hbm, table),
            (coupling_hbm, coupling),
            (index_hbm, index),
            (mask_hbm, mask),
        )
    ):
        load = pltpu.make_async_copy(source, target, in_sem.at[j])
        load.start()
        loads.append(load)

    stores = []

    def store_out(source, target):
        store = pltpu.make_async_copy(source, target, out_sem.at[len(stores)])
        store.start()
        stores.append(store)

    def flipped(apart):
        out, bit = me, 1
        while bit <= apart:
            if apart & bit:
                out = out + bit - 2 * bit * lax.rem(out // bit, 2)
            bit *= 2
        return out

    groups = PARTNERS
    barrier = pltpu.get_barrier_semaphore()
    total = 0
    for group in groups:
        for apart in group:
            pl.semaphore_signal(barrier, 1, device_id={"leaf": flipped(apart)})
            total += 1
    for peer in (after, before):
        pl.semaphore_signal(barrier, 1, device_id={"leaf": peer})
        total += 1
    for d in range(1, blocks):
        pl.semaphore_signal(barrier, 1, device_id={"blk": lax.rem(blk + d, blocks)})
        total += 1

    used = [0, 0]

    def start_exchange(step, terms):
        firsts = []
        for term in terms:
            send[used[0]] = pack(term)
            firsts.append(used[0])
            used[0] += 1
        started = []
        for j, apart in enumerate(groups[step]):
            parts = firsts if j == 0 else firsts[-1:]
            for source in parts:
                at = used[1]
                used[1] += 1
                copy = pltpu.make_async_remote_copy(
                    src_ref=send.at[source],
                    dst_ref=recv.at[at],
                    send_sem=send_sem.at[at],
                    recv_sem=recv_sem.at[at],
                    device_id={"leaf": flipped(apart)},
                )
                copy.start()
                started.append((copy, source, at))
        return started

    def finish_exchange(started):
        sums = {}
        for copy, source, at in started:
            copy.wait_recv()
            sums[source] = sums.get(source, send[source]) + recv[at]
        return [unpack(sums[s]) for s in sorted(sums)]

    grams, going, paths = [], [], {}

    def advance():
        grams.extend(finish_exchange(going[-1]))
        if len(going) < len(groups):
            at = paths[len(going)]
            terms = [carry((path[at], None), grams[-1])]
            if len(groups[len(going)]) > 1:
                terms.append(carry((path[at + 1], path[at + 2]), grams[-1]))
            going.append(start_exchange(len(going), terms))

    identity = eye(size)
    for i in range(leaves + inner):
        work[i, :, size : 2 * size] = identity
    loads[0].wait()
    for i in range(leaves):
        work[i, :, 0:size] = dot_nt(basis[i], basis[i])
    for j in (1, 2, 3):
        loads[j].wait()
    for m in range(leaves // 2):
        a, b = pairing[0, 2 * m], pairing[0, 2 * m + 1]
        work[leaves + m, :, 0:size] = carry(split(leaf_move[a]), work[a, :, 0:size]) + carry(
            split(leaf_move[b]), work[b, :, 0:size]
        )
    below, count = 0, leaves // 2
    while count > 1:
        for m in range(count // 2):
            a = below + 2 * m
            work[leaves + below + count + m, :, 0:size] = carry(
                split(inner_move[a]), work[leaves + a, :, 0:size]
            ) + carry(split(inner_move[a + 1]), work[leaves + a + 1, :, 0:size])
        below, count = below + count, count // 2
    root = carry(split(inner_move[inner - 1]), work[leaves + inner - 1, :, 0:size])
    pl.semaphore_wait(barrier, total)
    going.append(start_exchange(0, [root]))
    for j in (4, 5, 6, 7):
        loads[j].wait()
    level = lax.broadcasted_iota(jnp.int32, (8, n_leaf), 0)
    column = lax.broadcasted_iota(jnp.int32, (8, n_leaf), 1)
    choose = jnp.zeros((8, n_leaf), F32)
    for j in range(1, depth):
        owner = me // (1 << j) * (1 << j) + (1 << (j - 1))
        choose = jnp.where((level == j - 1) & (column == owner), 1.0, choose)
    choose = choose.astype(BF16)
    for b in range(size // 2):
        both = jnp.concatenate([table[b], table[size // 2 + b]], axis=0)
        moves[:, b, :] = dot_nt(choose, both)[: depth - 1]
    at, j = 0, 0
    for step in range(1, len(groups)):
        paths[step] = at
        near = unpack(moves[j]).astype(BF16)
        path[at] = near
        at, j = at + 1, j + 1
        if len(groups[step]) > 1:
            far_h, far_l = split(dot_nn(near, unpack(moves[j]).astype(BF16)))
            path[at] = far_h
            path[at + 1] = far_l
            at, j = at + 2, j + 1

    rows = 16
    for k in range(0, size, rows):
        factor_panel(work, done, 0, leaves + inner, rows, k, panel_chain)
        if k % (2 * rows) == 0:
            advance()

    keep = upper_mask(size)
    for i in range(leaves):
        low = jnp.where(keep, done[i, :, 0:size], 0.0)
        extended[halo + i] = low.astype(BF16)
        packed[halo + i] = pack(low).astype(BF16)
    halo_copies = []
    for j, (peer, source, target) in enumerate(((after, leaves, 0), (before, halo, halo + leaves))):
        copy = pltpu.make_async_remote_copy(
            src_ref=packed.at[pl.ds(source, halo)],
            dst_ref=packed.at[pl.ds(target, halo)],
            send_sem=halo_send_sem.at[j],
            recv_sem=halo_recv_sem.at[j],
            device_id={"leaf": peer},
        )
        copy.start()
        halo_copies.append(copy)

    advance()
    for t in range(leaves):
        for s in range(slots):
            half_ref[t, s] = dot_nn(extended[halo + t], coupling[t, s]).astype(BF16)
    begin = pl.multiple_of(blk * part, part)
    for i in range(leaves):
        weights = (math.sqrt(panels) * done[i, :, size : 2 * size]).astype(BF16)
        q_out[i] = dot_nn(weights, basis[i, :, pl.ds(begin, part)]).astype(BF16)
    for i in range(inner):
        inner_out[i] = jnp.where(keep, done[leaves + i, :, 0:size], 0.0)
    store_out(q_out, q_hbm)
    store_out(inner_out, inner_hbm)

    advance()
    for copy in halo_copies:
        copy.wait_recv()
    for i in range(halo):
        extended[i] = unpack(packed[i])
        extended[halo + leaves + i] = unpack(packed[halo + leaves + i])
    per = leaves // blocks
    base = me * leaves - halo
    row_scale = 1.0 / (slots * blocks * size)
    row_copies = []
    for d in range(1, blocks + 1):
        peer = lax.rem(blk + d, blocks)
        for i in range(per):
            t = peer * per + i
            square = None
            for s in range(slots):
                source = jnp.clip(index[s, t] - base, 0, leaves + 2 * halo - 1)
                full = dot_nt(half_ref[t, s], extended[source])
                value = (full * mask[s, t].astype(F32)).astype(BF16)
                projected[t, s] = value
                term = dot_nt(value, value)
                square = term if square is None else square + term
            squares[d - 1, i] = square * row_scale
        if d < blocks:
            for i in range(per):
                row_send[d - 1, i] = pack(squares[d - 1, i]).astype(BF16)
            copy = pltpu.make_async_remote_copy(
                src_ref=row_send.at[d - 1],
                dst_ref=row_recv.at[d - 1],
                send_sem=row_send_sem.at[d - 1],
                recv_sem=row_recv_sem.at[d - 1],
                device_id={"blk": peer},
            )
            copy.start()
            row_copies.append(copy)
    store_out(projected, projected_hbm)
    advance()
    for i in range(depth):
        work[i, :, 0:size] = grams[i]
        work[i, :, size : 2 * size] = jnp.zeros((size, size), F32)
    rows = 8
    for k in range(0, size, rows):
        factor_panel(work, done, 0, depth, rows, k, panel_ahead)
    for i in range(depth):
        upper_out[i] = jnp.where(keep, done[i, :, 0:size], 0.0)
    store_out(upper_out, upper_hbm)
    for copy in row_copies:
        copy.wait_recv()
    for i in range(per):
        square = row_recv[0, i].astype(F32)
        for d in range(1, blocks - 1):
            square = square + row_recv[d, i].astype(F32)
        weight_out[i] = squares[blocks - 1, i] + unpack(square)
    store_out(weight_out, weight_hbm)
    for started in going:
        for copy, _, _ in started:
            copy.wait_send()
    for copy in halo_copies + row_copies:
        copy.wait_send()
    for store in stores:
        store.wait()


def last_kernel(*refs):
    count = (len(refs) - 2) // 3
    in_sem, out_sem = refs[3 * count :]
    loads, stores = [], []
    for j in range(count):
        held = refs[2 * count + j]
        loads.append(pltpu.make_async_copy(refs[j], held, in_sem.at[j]))
        stores.append(pltpu.make_async_copy(held, refs[count + j], out_sem.at[j]))
        loads[-1].start()
    for load, store in zip(loads, stores):
        load.wait()
        store.start()
    for store in stores:
        store.wait()


def local(
    leaf_basis,
    leaf_pairing,
    leaf_transfer,
    inner_transfer,
    upper_transfer,
    coupling,
    source_cluster_index,
    coupling_slot_mask,
):
    leaves, size, panels = leaf_basis.shape
    inner = inner_transfer.shape[1]
    n_leaf, blocks = lax.axis_size("leaf"), lax.axis_size("blk")
    depth = n_leaf.bit_length() - 1
    slots = coupling.shape[1]
    part = panels // blocks
    anywhere = pl.BlockSpec(memory_space=pl.ANY)

    n_recv = sum(1 if len(group) == 1 else 4 for group in PARTNERS)
    n_send = sum(1 if len(group) == 1 else 2 for group in PARTNERS)
    n_path = sum(1 if len(group) == 1 else 3 for group in PARTNERS[1:])
    q_shape = jax.ShapeDtypeStruct((leaves, size, part), BF16)
    inner_shape = jax.ShapeDtypeStruct((inner, size, size), F32)
    upper_shape = jax.ShapeDtypeStruct((depth, size, size), F32)
    projected_shape = jax.ShapeDtypeStruct(coupling.shape, BF16)
    weight_shape = jax.ShapeDtypeStruct((leaves // blocks, size, size), F32)
    shapes = (q_shape, inner_shape, upper_shape, projected_shape, weight_shape)
    results = pl.pallas_call(
        tree_kernel,
        out_shape=shapes,
        in_specs=[anywhere] * 8,
        out_specs=(anywhere,) * 5,
        scratch_shapes=[
            VMEM(q_shape.shape, BF16),
            VMEM(inner_shape.shape, F32),
            VMEM(upper_shape.shape, F32),
            VMEM(coupling.shape, BF16),
            VMEM(weight_shape.shape, F32),
            SMEM((1, leaves), jnp.int32),
            VMEM((leaves, size, panels), BF16),
            VMEM((leaves, size, size), F32),
            VMEM((inner, size, size), F32),
            VMEM((size, size, n_leaf), BF16),
            VMEM((depth - 1, size // 2, 2 * size), F32),
            VMEM((n_path, size, size), BF16),
            VMEM(coupling.shape, BF16),
            SMEM((slots, leaves), jnp.int32),
            SMEM((slots, leaves), jnp.int32),
            VMEM((leaves + inner, size, 2 * size), F32),
            VMEM((leaves + inner, size, 2 * size), F32),
            VMEM((2 * leaves, size, size), BF16),
            VMEM((2 * leaves, size // 2, 2 * size), BF16),
            VMEM((leaves, slots, size, size), BF16),
            VMEM((blocks, leaves // blocks, size, size), F32),
            VMEM((n_send, size // 2, 2 * size), F32),
            VMEM((n_recv, size // 2, 2 * size), F32),
            VMEM((blocks - 1, leaves // blocks, size // 2, 2 * size), BF16),
            VMEM((blocks - 1, leaves // blocks, size // 2, 2 * size), BF16),
            pltpu.SemaphoreType.DMA((8,)),
            pltpu.SemaphoreType.DMA((5,)),
            pltpu.SemaphoreType.DMA((n_recv,)),
            pltpu.SemaphoreType.DMA((n_recv,)),
            pltpu.SemaphoreType.DMA((2,)),
            pltpu.SemaphoreType.DMA((2,)),
            pltpu.SemaphoreType.DMA((blocks - 1,)),
            pltpu.SemaphoreType.DMA((blocks - 1,)),
        ],
        compiler_params=pltpu.CompilerParams(
            collective_id=0, has_side_effects=True, vmem_limit_bytes=60 * 2**20
        ),
    )(
        leaf_pairing,
        leaf_basis,
        leaf_transfer,
        inner_transfer[0],
        jnp.transpose(upper_transfer, (1, 2, 0)),
        coupling,
        source_cluster_index.T,
        coupling_slot_mask.T,
    )

    q, inner_factor, upper_factor, projected, row_weight = pl.pallas_call(
        last_kernel,
        out_shape=shapes,
        in_specs=[anywhere] * 5,
        out_specs=(anywhere,) * 5,
        scratch_shapes=[VMEM(shape.shape, shape.dtype) for shape in shapes]
        + [pltpu.SemaphoreType.DMA((5,)), pltpu.SemaphoreType.DMA((5,))],
        compiler_params=pltpu.CompilerParams(vmem_limit_bytes=60 * 2**20),
    )(*results)
    return (q, inner_factor[None], upper_factor[None], projected, row_weight)


def solution(mesh):
    placed = (
        P("leaf", None, None),
        P("leaf", None),
        P("leaf", None, None),
        P("leaf", None, None, None),
        P(),
        P("leaf", "blk", None, None),
        P("leaf", "blk"),
        P("leaf", "blk"),
    )
    return jax.shard_map(
        local,
        mesh=mesh,
        in_specs=placed,
        out_specs=(
            P("leaf", None, "blk"),
            P("leaf", None, None, None),
            P("leaf", None, None, None),
            P("leaf", "blk", None, None),
            P(("leaf", "blk"), None, None),
        ),
        check_vma=False,
    )
```

```python
import functools
import math

import jax
import jax.numpy as jnp
from jax import lax
from jax.experimental import pallas as pl
from jax.experimental.pallas import tpu as pltpu
from jax.sharding import PartitionSpec as P

F32 = jnp.float32
BF16 = jnp.bfloat16
VMEM = pltpu.VMEM
SMEM = pltpu.SMEM
SPLIT = (1, 2)


def split(x):
    high = x.astype(BF16)
    return high, (x - high.astype(F32)).astype(BF16)


def dot_nn(a, b):
    return lax.dot_general(a, b, (((1,), (0,)), ((), ())), preferred_element_type=F32)


def dot_nt(a, b):
    return lax.dot_general(a, b, (((1,), (1,)), ((), ())), preferred_element_type=F32)


def dot_tn(a, b):
    return lax.dot_general(a, b, (((0,), (0,)), ((), ())), preferred_element_type=F32)


def carry(move, gram):
    move_h, move_l = move
    gram_h, gram_l = split(gram)
    right = dot_nn(gram_h, move_h) + dot_nn(gram_l, move_h)
    if move_l is not None:
        right = right + dot_nn(gram_h, move_l)
    right_h, right_l = split(right)
    out = dot_tn(move_h, right_h) + dot_tn(move_h, right_l)
    if move_l is not None:
        out = out + dot_tn(move_l, right_h)
    return out


def panel_chain(panel, start):
    count, rows, _ = panel.shape
    sub = lax.broadcasted_iota(jnp.int32, (1, rows, 128), 1)
    scale = jnp.zeros((count, rows, 128), F32)
    for r in range(rows):
        col = jnp.broadcast_to(panel[:, :, start + r : start + r + 1], panel.shape)
        inv = lax.rsqrt(col[:, r : r + 1, :])
        outer = jnp.where(sub > r, col, 0.0) * panel[:, r : r + 1, :]
        panel = panel - outer * (inv * inv)
        scale = jnp.where(sub == r, inv, scale)
    return panel * scale


def panel_ahead(panel, start):
    count, rows, _ = panel.shape
    sub = lax.broadcasted_iota(jnp.int32, (1, rows, 128), 1)
    scale = jnp.zeros((count, rows, 128), F32)
    cols = [
        jnp.broadcast_to(panel[:, :, start + r : start + r + 1], panel.shape) for r in range(rows)
    ]
    for r in range(rows):
        inv = lax.rsqrt(cols[r][:, r : r + 1, :])
        mult = jnp.where(sub > r, cols[r], 0.0) * (inv * inv)
        panel = panel - mult * panel[:, r : r + 1, :]
        for t in range(r + 1, rows):
            cols[t] = cols[t] - mult * cols[t][:, r : r + 1, :]
        scale = jnp.where(sub == r, inv, scale)
    return panel * scale


def factor_panel(work, done, first, count, rows, k, eliminate):
    size = work.shape[1]
    last = first + count
    panel = eliminate(work[first:last, k : k + rows, :], k)
    done[first:last, k : k + rows, :] = panel
    if k + rows < size:
        high, low = split(panel)
        left = jnp.concatenate([high, low, high], axis=1)
        right = jnp.concatenate([high, high, low], axis=1)
        for i in range(count):
            down = dot_tn(left[i], right[i])
            work[first + i, k + rows : size, :] = (
                work[first + i, k + rows : size, :] - down[k + rows : size, :]
            )


def upper_mask(size):
    return lax.broadcasted_iota(jnp.int32, (size, size), 0) <= lax.broadcasted_iota(
        jnp.int32, (size, size), 1
    )


def eye(size):
    return (
        lax.broadcasted_iota(jnp.int32, (size, size), 0)
        == lax.broadcasted_iota(jnp.int32, (size, size), 1)
    ).astype(F32)


def pack(matrix):
    half = matrix.shape[0] // 2
    return jnp.concatenate([matrix[:half], matrix[half:]], axis=1)


def unpack(packed):
    half = packed.shape[1] // 2
    return jnp.concatenate([packed[:, :half], packed[:, half:]], axis=0)


def tree_kernel(
    pairing_hbm,
    basis_hbm,
    leaf_move_hbm,
    inner_move_hbm,
    table_hbm,
    coupling_hbm,
    index_hbm,
    mask_hbm,
    q_hbm,
    inner_hbm,
    upper_hbm,
    projected_hbm,
    weight_hbm,
    q_out,
    inner_out,
    upper_out,
    projected,
    weight_out,
    pairing,
    basis,
    leaf_move,
    inner_move,
    table,
    moves,
    path,
    coupling,
    index,
    mask,
    work,
    done,
    extended,
    packed,
    half_ref,
    squares,
    send,
    recv,
    gathered,
    row_send,
    row_recv,
    in_sem,
    out_sem,
    send_sem,
    recv_sem,
    halo_send_sem,
    halo_recv_sem,
    row_send_sem,
    row_recv_sem,
    gather_send_sem,
    gather_recv_sem,
):
    leaves, size, panels = basis.shape
    inner = inner_move.shape[0]
    slots = coupling.shape[1]
    part = q_out.shape[2]
    halo = leaves // 2
    n_leaf, blocks = lax.axis_size("leaf"), lax.axis_size("blk")
    me, blk = lax.axis_index("leaf"), lax.axis_index("blk")
    after, before = lax.rem(me + 1, n_leaf), lax.rem(me + n_leaf - 1, n_leaf)
    depth = upper_out.shape[0]

    loads = []
    for j, (source, target) in enumerate(
        (
            (basis_hbm, basis),
            (pairing_hbm, pairing),
            (leaf_move_hbm, leaf_move),
            (inner_move_hbm, inner_move),
            (table_hbm, table),
            (coupling_hbm, coupling),
            (index_hbm, index),
            (mask_hbm, mask),
        )
    ):
        load = pltpu.make_async_copy(source, target, in_sem.at[j])
        load.start()
        loads.append(load)

    stores = []

    def store_out(source, target):
        store = pltpu.make_async_copy(source, target, out_sem.at[len(stores)])
        store.start()
        stores.append(store)

    def flipped(apart):
        out, bit = me, 1
        while bit <= apart:
            if apart & bit:
                out = out + bit - 2 * bit * lax.rem(out // bit, 2)
            bit *= 2
        return out

    groups = [(1,)] + [(2 << (2 * g), 4 << (2 * g), 6 << (2 * g)) for g in range((depth - 1) // 2)]
    barrier = pltpu.get_barrier_semaphore()
    total = 0
    for group in groups:
        for apart in group:
            pl.semaphore_signal(barrier, 1, device_id={"leaf": flipped(apart)})
            total += 1
    for peer in (after, before):
        pl.semaphore_signal(barrier, 1, device_id={"leaf": peer})
        total += 1
    for d in range(1, blocks):
        pl.semaphore_signal(barrier, 1, device_id={"blk": lax.rem(blk + d, blocks)})
        total += 1

    share = size // 2 // blocks
    quarter = pl.ds(pl.multiple_of(blk * share, share), share)
    used = [0, 0]

    def start_exchange(step, terms):
        firsts = []
        for term in terms:
            send[used[0]] = pack(term)
            firsts.append(used[0])
            used[0] += 1
        started = []
        for j, apart in enumerate(groups[step]):
            parts = firsts if j == 0 else firsts[-1:]
            for source in parts:
                at = used[1]
                used[1] += 1
                rows = quarter if step in SPLIT else pl.ds(0, size // 2)
                copy = pltpu.make_async_remote_copy(
                    src_ref=send.at[source, rows],
                    dst_ref=recv.at[at, rows],
                    send_sem=send_sem.at[at],
                    recv_sem=recv_sem.at[at],
                    device_id={"leaf": flipped(apart)},
                )
                copy.start()
                started.append((copy, source, at))
        return started

    gathers = []

    def start_gather(started):
        sums = {}
        for copy, source, at in started:
            copy.wait_recv()
            sums[source] = sums.get(source, send[source, quarter, :]) + recv[at, quarter, :]
        first = 2 * len(gathers)
        copies = []
        for j, source in enumerate(sorted(sums)):
            gathered[first + j, quarter, :] = sums[source]
            for d in range(1, blocks):
                at = (first + j) * (blocks - 1) + d - 1
                copy = pltpu.make_async_remote_copy(
                    src_ref=gathered.at[first + j, quarter],
                    dst_ref=gathered.at[first + j, quarter],
                    send_sem=gather_send_sem.at[at],
                    recv_sem=gather_recv_sem.at[at],
                    device_id={"blk": lax.rem(blk + d, blocks)},
                )
                copy.start()
                copies.append(copy)
        gathers.append((copies, len(sums)))

    def finish_gather():
        copies, count = gathers[-1]
        for copy in copies:
            copy.wait_recv()
        return [unpack(gathered[2 * (len(gathers) - 1) + j]) for j in range(count)]

    def finish_exchange(started):
        sums = {}
        for copy, source, at in started:
            copy.wait_recv()
            sums[source] = sums.get(source, send[source]) + recv[at]
        return [unpack(sums[s]) for s in sorted(sums)]

    grams, going = [], []

    def advance():
        if len(going) - 1 in SPLIT:
            grams.extend(finish_gather())
        else:
            grams.extend(finish_exchange(going[-1]))
        if len(going) < len(groups):
            at = 3 * (len(going) - 1)
            terms = [
                carry((path[at], None), grams[-1]),
                carry((path[at + 1], path[at + 2]), grams[-1]),
            ]
            going.append(start_exchange(len(going), terms))

    identity = eye(size)
    for i in range(leaves + inner):
        work[i, :, size : 2 * size] = identity
    loads[0].wait()
    for i in range(leaves):
        work[i, :, 0:size] = dot_nt(basis[i], basis[i])
    for j in (1, 2, 3):
        loads[j].wait()
    for m in range(leaves // 2):
        a, b = pairing[0, 2 * m], pairing[0, 2 * m + 1]
        work[leaves + m, :, 0:size] = carry(split(leaf_move[a]), work[a, :, 0:size]) + carry(
            split(leaf_move[b]), work[b, :, 0:size]
        )
    below, count = 0, leaves // 2
    while count > 1:
        for m in range(count // 2):
            a = below + 2 * m
            work[leaves + below + count + m, :, 0:size] = carry(
                split(inner_move[a]), work[leaves + a, :, 0:size]
            ) + carry(split(inner_move[a + 1]), work[leaves + a + 1, :, 0:size])
        below, count = below + count, count // 2
    root = carry(split(inner_move[inner - 1]), work[leaves + inner - 1, :, 0:size])
    pl.semaphore_wait(barrier, total)
    going.append(start_exchange(0, [root]))
    for j in (4, 5, 6, 7):
        loads[j].wait()
    level = lax.broadcasted_iota(jnp.int32, (8, n_leaf), 0)
    column = lax.broadcasted_iota(jnp.int32, (8, n_leaf), 1)
    choose = jnp.zeros((8, n_leaf), F32)
    for j in range(1, depth):
        owner = me // (1 << j) * (1 << j) + (1 << (j - 1))
        choose = jnp.where((level == j - 1) & (column == owner), 1.0, choose)
    choose = choose.astype(BF16)
    for b in range(size // 2):
        both = jnp.concatenate([table[b], table[size // 2 + b]], axis=0)
        moves[:, b, :] = dot_nt(choose, both)[: depth - 1]
    for j in range(len(groups) - 1):
        near = unpack(moves[2 * j]).astype(BF16)
        path[3 * j] = near
        far_h, far_l = split(dot_nn(near, unpack(moves[2 * j + 1]).astype(BF16)))
        path[3 * j + 1] = far_h
        path[3 * j + 2] = far_l

    rows = 16
    for k in range(0, size, rows):
        factor_panel(work, done, 0, leaves + inner, rows, k, panel_chain)
        if k in (0, 2 * rows):
            advance()
        if k == rows:
            start_gather(going[-1])

    keep = upper_mask(size)
    for i in range(leaves):
        low = jnp.where(keep, done[i, :, 0:size], 0.0)
        extended[halo + i] = low.astype(BF16)
        packed[halo + i] = pack(low).astype(BF16)
    halo_copies = []
    for j, (peer, source, target) in enumerate(((after, leaves, 0), (before, halo, halo + leaves))):
        copy = pltpu.make_async_remote_copy(
            src_ref=packed.at[pl.ds(source, halo)],
            dst_ref=packed.at[pl.ds(target, halo)],
            send_sem=halo_send_sem.at[j],
            recv_sem=halo_recv_sem.at[j],
            device_id={"leaf": peer},
        )
        copy.start()
        halo_copies.append(copy)

    start_gather(going[-1])
    for t in range(leaves):
        for s in range(slots):
            half_ref[t, s] = dot_nn(extended[halo + t], coupling[t, s]).astype(BF16)
    begin = pl.multiple_of(blk * part, part)
    for i in range(leaves):
        weights = (math.sqrt(panels) * done[i, :, size : 2 * size]).astype(BF16)
        q_out[i] = dot_nn(weights, basis[i, :, pl.ds(begin, part)]).astype(BF16)
    for i in range(inner):
        inner_out[i] = jnp.where(keep, done[leaves + i, :, 0:size], 0.0)
    store_out(q_out, q_hbm)
    store_out(inner_out, inner_hbm)

    advance()
    for copy in halo_copies:
        copy.wait_recv()
    for i in range(halo):
        extended[i] = unpack(packed[i])
        extended[halo + leaves + i] = unpack(packed[halo + leaves + i])
    per = leaves // blocks
    base = me * leaves - halo
    row_scale = 1.0 / (slots * blocks * size)
    row_copies = []
    for d in range(1, blocks + 1):
        peer = lax.rem(blk + d, blocks)
        for i in range(per):
            t = peer * per + i
            square = None
            for s in range(slots):
                source = jnp.clip(index[s, t] - base, 0, leaves + 2 * halo - 1)
                full = dot_nt(half_ref[t, s], extended[source])
                value = (full * mask[s, t].astype(F32)).astype(BF16)
                projected[t, s] = value
                term = dot_nt(value, value)
                square = term if square is None else square + term
            squares[d - 1, i] = square * row_scale
        if d < blocks:
            for i in range(per):
                row_send[d - 1, i] = pack(squares[d - 1, i]).astype(BF16)
            copy = pltpu.make_async_remote_copy(
                src_ref=row_send.at[d - 1],
                dst_ref=row_recv.at[d - 1],
                send_sem=row_send_sem.at[d - 1],
                recv_sem=row_recv_sem.at[d - 1],
                device_id={"blk": peer},
            )
            copy.start()
            row_copies.append(copy)
    store_out(projected, projected_hbm)
    advance()
    for i in range(depth):
        work[i, :, 0:size] = grams[i]
        work[i, :, size : 2 * size] = jnp.zeros((size, size), F32)
    rows = 8
    for k in range(0, size, rows):
        factor_panel(work, done, 0, depth, rows, k, panel_ahead)
    for i in range(depth):
        upper_out[i] = jnp.where(keep, done[i, :, 0:size], 0.0)
    store_out(upper_out, upper_hbm)
    for copy in row_copies:
        copy.wait_recv()
    for i in range(per):
        square = row_recv[0, i].astype(F32)
        for d in range(1, blocks - 1):
            square = square + row_recv[d, i].astype(F32)
        weight_out[i] = squares[blocks - 1, i] + unpack(square)
    store_out(weight_out, weight_hbm)
    for started in going:
        for copy, _, _ in started:
            copy.wait_send()
    for copy in halo_copies + row_copies + [c for copies, _ in gathers for c in copies]:
        copy.wait_send()
    for store in stores:
        store.wait()


def last_kernel(*refs):
    count = (len(refs) - 2) // 3
    in_sem, out_sem = refs[3 * count :]
    loads, stores = [], []
    for j in range(count):
        held = refs[2 * count + j]
        loads.append(pltpu.make_async_copy(refs[j], held, in_sem.at[j]))
        stores.append(pltpu.make_async_copy(held, refs[count + j], out_sem.at[j]))
        loads[-1].start()
    for load, store in zip(loads, stores):
        load.wait()
        store.start()
    for store in stores:
        store.wait()


def local(
    leaf_basis,
    leaf_pairing,
    leaf_transfer,
    inner_transfer,
    upper_transfer,
    coupling,
    source_cluster_index,
    coupling_slot_mask,
):
    leaves, size, panels = leaf_basis.shape
    inner = inner_transfer.shape[1]
    n_leaf, blocks = lax.axis_size("leaf"), lax.axis_size("blk")
    depth = n_leaf.bit_length() - 1
    slots = coupling.shape[1]
    part = panels // blocks
    anywhere = pl.BlockSpec(memory_space=pl.ANY)

    n_recv = 1 + 4 * ((depth - 1) // 2)
    n_send = 1 + 2 * ((depth - 1) // 2)
    q_shape = jax.ShapeDtypeStruct((leaves, size, part), BF16)
    inner_shape = jax.ShapeDtypeStruct((inner, size, size), F32)
    upper_shape = jax.ShapeDtypeStruct((depth, size, size), F32)
    projected_shape = jax.ShapeDtypeStruct(coupling.shape, BF16)
    weight_shape = jax.ShapeDtypeStruct((leaves // blocks, size, size), F32)
    shapes = (q_shape, inner_shape, upper_shape, projected_shape, weight_shape)
    results = pl.pallas_call(
        tree_kernel,
        out_shape=shapes,
        in_specs=[anywhere] * 8,
        out_specs=(anywhere,) * 5,
        scratch_shapes=[
            VMEM(q_shape.shape, BF16),
            VMEM(inner_shape.shape, F32),
            VMEM(upper_shape.shape, F32),
            VMEM(coupling.shape, BF16),
            VMEM(weight_shape.shape, F32),
            SMEM((1, leaves), jnp.int32),
            VMEM((leaves, size, panels), BF16),
            VMEM((leaves, size, size), F32),
            VMEM((inner, size, size), F32),
            VMEM((size, size, n_leaf), BF16),
            VMEM((depth - 1, size // 2, 2 * size), F32),
            VMEM((3 * ((depth - 1) // 2), size, size), BF16),
            VMEM(coupling.shape, BF16),
            SMEM((slots, leaves), jnp.int32),
            SMEM((slots, leaves), jnp.int32),
            VMEM((leaves + inner, size, 2 * size), F32),
            VMEM((leaves + inner, size, 2 * size), F32),
            VMEM((2 * leaves, size, size), BF16),
            VMEM((2 * leaves, size // 2, 2 * size), BF16),
            VMEM((leaves, slots, size, size), BF16),
            VMEM((blocks, leaves // blocks, size, size), F32),
            VMEM((n_send, size // 2, 2 * size), F32),
            VMEM((n_recv, size // 2, 2 * size), F32),
            VMEM((2 * len(SPLIT), size // 2, 2 * size), F32),
            VMEM((blocks - 1, leaves // blocks, size // 2, 2 * size), BF16),
            VMEM((blocks - 1, leaves // blocks, size // 2, 2 * size), BF16),
            pltpu.SemaphoreType.DMA((8,)),
            pltpu.SemaphoreType.DMA((5,)),
            pltpu.SemaphoreType.DMA((n_recv,)),
            pltpu.SemaphoreType.DMA((n_recv,)),
            pltpu.SemaphoreType.DMA((2,)),
            pltpu.SemaphoreType.DMA((2,)),
            pltpu.SemaphoreType.DMA((blocks - 1,)),
            pltpu.SemaphoreType.DMA((blocks - 1,)),
            pltpu.SemaphoreType.DMA((2 * len(SPLIT) * (blocks - 1),)),
            pltpu.SemaphoreType.DMA((2 * len(SPLIT) * (blocks - 1),)),
        ],
        compiler_params=pltpu.CompilerParams(
            collective_id=0, has_side_effects=True, vmem_limit_bytes=60 * 2**20
        ),
    )(
        leaf_pairing,
        leaf_basis,
        leaf_transfer,
        inner_transfer[0],
        jnp.transpose(upper_transfer, (1, 2, 0)),
        coupling,
        source_cluster_index.T,
        coupling_slot_mask.T,
    )

    q, inner_factor, upper_factor, projected, row_weight = pl.pallas_call(
        last_kernel,
        out_shape=shapes,
        in_specs=[anywhere] * 5,
        out_specs=(anywhere,) * 5,
        scratch_shapes=[VMEM(shape.shape, shape.dtype) for shape in shapes]
        + [pltpu.SemaphoreType.DMA((5,)), pltpu.SemaphoreType.DMA((5,))],
        compiler_params=pltpu.CompilerParams(vmem_limit_bytes=60 * 2**20),
    )(*results)
    return (q, inner_factor[None], upper_factor[None], projected, row_weight)


def solution(mesh):
    placed = (
        P("leaf", None, None),
        P("leaf", None),
        P("leaf", None, None),
        P("leaf", None, None, None),
        P(),
        P("leaf", "blk", None, None),
        P("leaf", "blk"),
        P("leaf", "blk"),
    )
    return jax.shard_map(
        local,
        mesh=mesh,
        in_specs=placed,
        out_specs=(
            P("leaf", None, "blk"),
            P("leaf", None, None, None),
            P("leaf", None, None, None),
            P("leaf", "blk", None, None),
            P(("leaf", "blk"), None, None),
        ),
        check_vma=False,
    )
```

```python
import functools
import math

import jax
import jax.numpy as jnp
from jax import lax
from jax.experimental import pallas as pl
from jax.experimental.pallas import tpu as pltpu
from jax.sharding import PartitionSpec as P

F32 = jnp.float32
BF16 = jnp.bfloat16
VMEM = pltpu.VMEM
SMEM = pltpu.SMEM


def split(x):
    high = x.astype(BF16)
    return high, (x - high.astype(F32)).astype(BF16)


def dot_nn(a, b):
    return lax.dot_general(a, b, (((1,), (0,)), ((), ())), preferred_element_type=F32)


def dot_nt(a, b):
    return lax.dot_general(a, b, (((1,), (1,)), ((), ())), preferred_element_type=F32)


def dot_tn(a, b):
    return lax.dot_general(a, b, (((0,), (0,)), ((), ())), preferred_element_type=F32)


def carry(move, gram):
    move_h, move_l = move
    gram_h, gram_l = split(gram)
    right = dot_nn(gram_h, move_h) + dot_nn(gram_l, move_h)
    if move_l is not None:
        right = right + dot_nn(gram_h, move_l)
    right_h, right_l = split(right)
    out = dot_tn(move_h, right_h) + dot_tn(move_h, right_l)
    if move_l is not None:
        out = out + dot_tn(move_l, right_h)
    return out


def panel_chain(panel, start):
    count, rows, _ = panel.shape
    sub = lax.broadcasted_iota(jnp.int32, (1, rows, 128), 1)
    scale = jnp.zeros((count, rows, 128), F32)
    for r in range(rows):
        col = jnp.broadcast_to(panel[:, :, start + r : start + r + 1], panel.shape)
        inv = lax.rsqrt(col[:, r : r + 1, :])
        outer = jnp.where(sub > r, col, 0.0) * panel[:, r : r + 1, :]
        panel = panel - outer * (inv * inv)
        scale = jnp.where(sub == r, inv, scale)
    return panel * scale


def panel_ahead(panel, start):
    count, rows, _ = panel.shape
    sub = lax.broadcasted_iota(jnp.int32, (1, rows, 128), 1)
    scale = jnp.zeros((count, rows, 128), F32)
    cols = [
        jnp.broadcast_to(panel[:, :, start + r : start + r + 1], panel.shape) for r in range(rows)
    ]
    for r in range(rows):
        inv = lax.rsqrt(cols[r][:, r : r + 1, :])
        mult = jnp.where(sub > r, cols[r], 0.0) * (inv * inv)
        panel = panel - mult * panel[:, r : r + 1, :]
        for t in range(r + 1, rows):
            cols[t] = cols[t] - mult * cols[t][:, r : r + 1, :]
        scale = jnp.where(sub == r, inv, scale)
    return panel * scale


def factor_panel(work, done, first, count, rows, k, eliminate):
    size = work.shape[1]
    last = first + count
    panel = eliminate(work[first:last, k : k + rows, :], k)
    done[first:last, k : k + rows, :] = panel
    if k + rows < size:
        high, low = split(panel)
        left = jnp.concatenate([high, low, high], axis=1)
        right = jnp.concatenate([high, high, low], axis=1)
        for i in range(count):
            down = dot_tn(left[i], right[i])
            work[first + i, k + rows : size, :] = (
                work[first + i, k + rows : size, :] - down[k + rows : size, :]
            )


def upper_mask(size):
    return lax.broadcasted_iota(jnp.int32, (size, size), 0) <= lax.broadcasted_iota(
        jnp.int32, (size, size), 1
    )


def eye(size):
    return (
        lax.broadcasted_iota(jnp.int32, (size, size), 0)
        == lax.broadcasted_iota(jnp.int32, (size, size), 1)
    ).astype(F32)


def pack(matrix):
    half = matrix.shape[0] // 2
    return jnp.concatenate([matrix[:half], matrix[half:]], axis=1)


def unpack(packed):
    half = packed.shape[1] // 2
    return jnp.concatenate([packed[:, :half], packed[:, half:]], axis=0)


def tree_kernel(
    pairing_hbm,
    basis_hbm,
    leaf_move_hbm,
    inner_move_hbm,
    table_hbm,
    coupling_hbm,
    index_hbm,
    mask_hbm,
    q_hbm,
    inner_hbm,
    gram_hbm,
    projected_hbm,
    weight_hbm,
    q_out,
    inner_out,
    gram_out,
    projected,
    weight_out,
    pairing,
    basis,
    leaf_move,
    inner_move,
    table,
    moves,
    path,
    coupling,
    index,
    mask,
    work,
    done,
    extended,
    packed,
    half_ref,
    squares,
    send,
    recv,
    row_send,
    row_recv,
    in_sem,
    out_sem,
    send_sem,
    recv_sem,
    halo_send_sem,
    halo_recv_sem,
    row_send_sem,
    row_recv_sem,
):
    leaves, size, panels = basis.shape
    inner = inner_move.shape[0]
    slots = coupling.shape[1]
    part = q_out.shape[2]
    halo = leaves // 2
    n_leaf, blocks = lax.axis_size("leaf"), lax.axis_size("blk")
    me, blk = lax.axis_index("leaf"), lax.axis_index("blk")
    after, before = lax.rem(me + 1, n_leaf), lax.rem(me + n_leaf - 1, n_leaf)
    depth = gram_out.shape[0]

    loads = []
    for j, (source, target) in enumerate(
        (
            (basis_hbm, basis),
            (pairing_hbm, pairing),
            (leaf_move_hbm, leaf_move),
            (inner_move_hbm, inner_move),
            (table_hbm, table),
            (coupling_hbm, coupling),
            (index_hbm, index),
            (mask_hbm, mask),
        )
    ):
        load = pltpu.make_async_copy(source, target, in_sem.at[j])
        load.start()
        loads.append(load)

    stores = []

    def store_out(source, target):
        store = pltpu.make_async_copy(source, target, out_sem.at[len(stores)])
        store.start()
        stores.append(store)

    def flipped(apart):
        out, bit = me, 1
        while bit <= apart:
            if apart & bit:
                out = out + bit - 2 * bit * lax.rem(out // bit, 2)
            bit *= 2
        return out

    groups = [(1,)] + [(2 << (2 * g), 4 << (2 * g), 6 << (2 * g)) for g in range((depth - 1) // 2)]
    barrier = pltpu.get_barrier_semaphore()
    total = 0
    for group in groups:
        for apart in group:
            pl.semaphore_signal(barrier, 1, device_id={"leaf": flipped(apart)})
            total += 1
    for peer in (after, before):
        pl.semaphore_signal(barrier, 1, device_id={"leaf": peer})
        total += 1
    for d in range(1, blocks):
        pl.semaphore_signal(barrier, 1, device_id={"blk": lax.rem(blk + d, blocks)})
        total += 1

    used = [0, 0]

    def start_exchange(step, terms):
        firsts = []
        for term in terms:
            send[used[0]] = pack(term)
            firsts.append(used[0])
            used[0] += 1
        started = []
        for j, apart in enumerate(groups[step]):
            parts = firsts if j == 0 else firsts[-1:]
            for source in parts:
                at = used[1]
                used[1] += 1
                copy = pltpu.make_async_remote_copy(
                    src_ref=send.at[source],
                    dst_ref=recv.at[at],
                    send_sem=send_sem.at[at],
                    recv_sem=recv_sem.at[at],
                    device_id={"leaf": flipped(apart)},
                )
                copy.start()
                started.append((copy, source, at))
        return started

    def finish_exchange(started):
        sums = {}
        for copy, source, at in started:
            copy.wait_recv()
            sums[source] = sums.get(source, send[source]) + recv[at]
        return [unpack(sums[s]) for s in sorted(sums)]

    grams, going = [], []

    def advance():
        grams.extend(finish_exchange(going[-1]))
        if len(going) < len(groups):
            at = 3 * (len(going) - 1)
            terms = [
                carry((path[at], None), grams[-1]),
                carry((path[at + 1], path[at + 2]), grams[-1]),
            ]
            going.append(start_exchange(len(going), terms))

    identity = eye(size)
    for i in range(leaves + inner):
        work[i, :, size : 2 * size] = identity
    loads[0].wait()
    for i in range(leaves):
        work[i, :, 0:size] = dot_nt(basis[i], basis[i])
    for j in (1, 2, 3):
        loads[j].wait()
    for m in range(leaves // 2):
        a, b = pairing[0, 2 * m], pairing[0, 2 * m + 1]
        work[leaves + m, :, 0:size] = carry(split(leaf_move[a]), work[a, :, 0:size]) + carry(
            split(leaf_move[b]), work[b, :, 0:size]
        )
    below, count = 0, leaves // 2
    while count > 1:
        for m in range(count // 2):
            a = below + 2 * m
            work[leaves + below + count + m, :, 0:size] = carry(
                split(inner_move[a]), work[leaves + a, :, 0:size]
            ) + carry(split(inner_move[a + 1]), work[leaves + a + 1, :, 0:size])
        below, count = below + count, count // 2
    root = carry(split(inner_move[inner - 1]), work[leaves + inner - 1, :, 0:size])
    pl.semaphore_wait(barrier, total)
    going.append(start_exchange(0, [root]))
    for j in (4, 5, 6, 7):
        loads[j].wait()
    level = lax.broadcasted_iota(jnp.int32, (8, n_leaf), 0)
    column = lax.broadcasted_iota(jnp.int32, (8, n_leaf), 1)
    choose = jnp.zeros((8, n_leaf), F32)
    for j in range(1, depth):
        owner = me // (1 << j) * (1 << j) + (1 << (j - 1))
        choose = jnp.where((level == j - 1) & (column == owner), 1.0, choose)
    choose = choose.astype(BF16)
    for b in range(size // 2):
        both = jnp.concatenate([table[b], table[size // 2 + b]], axis=0)
        moves[:, b, :] = dot_nt(choose, both)[: depth - 1]
    for j in range(len(groups) - 1):
        near = unpack(moves[2 * j]).astype(BF16)
        path[3 * j] = near
        far_h, far_l = split(dot_nn(near, unpack(moves[2 * j + 1]).astype(BF16)))
        path[3 * j + 1] = far_h
        path[3 * j + 2] = far_l

    rows = 16
    for k in range(0, size, rows):
        factor_panel(work, done, 0, leaves + inner, rows, k, panel_chain)
        if k % (2 * rows) == 0:
            advance()

    keep = upper_mask(size)
    for i in range(leaves):
        low = jnp.where(keep, done[i, :, 0:size], 0.0)
        extended[halo + i] = low.astype(BF16)
        packed[halo + i] = pack(low).astype(BF16)
    halo_copies = []
    for j, (peer, source, target) in enumerate(((after, leaves, 0), (before, halo, halo + leaves))):
        copy = pltpu.make_async_remote_copy(
            src_ref=packed.at[pl.ds(source, halo)],
            dst_ref=packed.at[pl.ds(target, halo)],
            send_sem=halo_send_sem.at[j],
            recv_sem=halo_recv_sem.at[j],
            device_id={"leaf": peer},
        )
        copy.start()
        halo_copies.append(copy)

    for t in range(leaves):
        for s in range(slots):
            half_ref[t, s] = dot_nn(extended[halo + t], coupling[t, s]).astype(BF16)
    begin = pl.multiple_of(blk * part, part)
    for i in range(leaves):
        weights = (math.sqrt(panels) * done[i, :, size : 2 * size]).astype(BF16)
        q_out[i] = dot_nn(weights, basis[i, :, pl.ds(begin, part)]).astype(BF16)
    for i in range(inner):
        inner_out[i] = jnp.where(keep, done[leaves + i, :, 0:size], 0.0)
    store_out(q_out, q_hbm)
    store_out(inner_out, inner_hbm)

    advance()
    for copy in halo_copies:
        copy.wait_recv()
    for i in range(halo):
        extended[i] = unpack(packed[i])
        extended[halo + leaves + i] = unpack(packed[halo + leaves + i])
    per = leaves // blocks
    base = me * leaves - halo
    row_scale = 1.0 / (slots * blocks * size)
    row_copies = []
    for d in range(1, blocks + 1):
        peer = lax.rem(blk + d, blocks)
        for i in range(per):
            t = peer * per + i
            square = None
            for s in range(slots):
                source = jnp.clip(index[s, t] - base, 0, leaves + 2 * halo - 1)
                full = dot_nt(half_ref[t, s], extended[source])
                value = (full * mask[s, t].astype(F32)).astype(BF16)
                projected[t, s] = value
                term = dot_nt(value, value)
                square = term if square is None else square + term
            squares[d - 1, i] = square * row_scale
        if d < blocks:
            for i in range(per):
                row_send[d - 1, i] = pack(squares[d - 1, i]).astype(BF16)
            copy = pltpu.make_async_remote_copy(
                src_ref=row_send.at[d - 1],
                dst_ref=row_recv.at[d - 1],
                send_sem=row_send_sem.at[d - 1],
                recv_sem=row_recv_sem.at[d - 1],
                device_id={"blk": peer},
            )
            copy.start()
            row_copies.append(copy)
    store_out(projected, projected_hbm)
    early = len(grams)
    for i in range(early):
        work[i, :, 0:size] = grams[i]
        work[i, :, size : 2 * size] = jnp.zeros((size, size), F32)
    rows = 8
    for k in range(0, size, rows):
        factor_panel(work, done, 0, early, rows, k, panel_ahead)
    for i in range(early):
        gram_out[i] = jnp.where(keep, done[i, :, 0:size], 0.0)
    advance()
    for i in range(early, depth):
        gram_out[i] = grams[i]
    store_out(gram_out, gram_hbm)
    for copy in row_copies:
        copy.wait_recv()
    for i in range(per):
        square = row_recv[0, i].astype(F32)
        for d in range(1, blocks - 1):
            square = square + row_recv[d, i].astype(F32)
        weight_out[i] = squares[blocks - 1, i] + unpack(square)
    store_out(weight_out, weight_hbm)
    for started in going:
        for copy, _, _ in started:
            copy.wait_send()
    for copy in halo_copies + row_copies:
        copy.wait_send()
    for store in stores:
        store.wait()


def last_kernel(
    gram_hbm,
    q,
    inner,
    projected,
    weight,
    upper_out,
    q_out,
    inner_out,
    projected_out,
    weight_out,
    gram,
    q_held,
    inner_held,
    projected_held,
    weight_held,
    work,
    done,
    gram_sem,
    in_sem,
    out_sem,
):
    depth, size, _ = gram.shape
    first = pltpu.make_async_copy(gram_hbm, gram, gram_sem)
    first.start()
    loads, stores = [], []
    for j, (source, held, target) in enumerate(
        (
            (projected, projected_held, projected_out),
            (q, q_held, q_out),
            (inner, inner_held, inner_out),
            (weight, weight_held, weight_out),
        )
    ):
        loads.append(pltpu.make_async_copy(source, held, in_sem.at[j]))
        stores.append(pltpu.make_async_copy(held, target, out_sem.at[j]))
        loads[-1].start()
    first.wait()
    late = work.shape[0]
    for i in range(depth - late):
        upper_out[i] = gram[i]
    for i in range(late):
        work[i, :, 0:size] = gram[depth - late + i]
        work[i, :, size : 2 * size] = jnp.zeros((size, size), F32)
    rows = 16
    for k in range(0, size, rows):
        factor_panel(work, done, 0, late, rows, k, panel_ahead)
        if k == rows:
            for load, store in zip(loads, stores):
                load.wait()
                store.start()
    keep = upper_mask(size)
    for i in range(late):
        upper_out[depth - late + i] = jnp.where(keep, done[i, :, 0:size], 0.0)
    for store in stores:
        store.wait()


def local(
    leaf_basis,
    leaf_pairing,
    leaf_transfer,
    inner_transfer,
    upper_transfer,
    coupling,
    source_cluster_index,
    coupling_slot_mask,
):
    leaves, size, panels = leaf_basis.shape
    inner = inner_transfer.shape[1]
    n_leaf, blocks = lax.axis_size("leaf"), lax.axis_size("blk")
    depth = n_leaf.bit_length() - 1
    slots = coupling.shape[1]
    part = panels // blocks
    vmem = pl.BlockSpec(memory_space=VMEM)
    anywhere = pl.BlockSpec(memory_space=pl.ANY)

    n_recv = 1 + 4 * ((depth - 1) // 2)
    n_send = 1 + 2 * ((depth - 1) // 2)
    q_shape = jax.ShapeDtypeStruct((leaves, size, part), BF16)
    inner_shape = jax.ShapeDtypeStruct((inner, size, size), F32)
    upper_shape = jax.ShapeDtypeStruct((depth, size, size), F32)
    projected_shape = jax.ShapeDtypeStruct(coupling.shape, BF16)
    weight_shape = jax.ShapeDtypeStruct((leaves // blocks, size, size), F32)
    q, inner_factor, upper_gram, projected, row_weight = pl.pallas_call(
        tree_kernel,
        out_shape=(q_shape, inner_shape, upper_shape, projected_shape, weight_shape),
        in_specs=[anywhere] * 8,
        out_specs=(anywhere,) * 5,
        scratch_shapes=[
            VMEM(q_shape.shape, BF16),
            VMEM(inner_shape.shape, F32),
            VMEM(upper_shape.shape, F32),
            VMEM(coupling.shape, BF16),
            VMEM(weight_shape.shape, F32),
            SMEM((1, leaves), jnp.int32),
            VMEM((leaves, size, panels), BF16),
            VMEM((leaves, size, size), F32),
            VMEM((inner, size, size), F32),
            VMEM((size, size, n_leaf), BF16),
            VMEM((depth - 1, size // 2, 2 * size), F32),
            VMEM((3 * ((depth - 1) // 2), size, size), BF16),
            VMEM(coupling.shape, BF16),
            SMEM((slots, leaves), jnp.int32),
            SMEM((slots, leaves), jnp.int32),
            VMEM((leaves + inner, size, 2 * size), F32),
            VMEM((leaves + inner, size, 2 * size), F32),
            VMEM((2 * leaves, size, size), BF16),
            VMEM((2 * leaves, size // 2, 2 * size), BF16),
            VMEM((leaves, slots, size, size), BF16),
            VMEM((blocks, leaves // blocks, size, size), F32),
            VMEM((n_send, size // 2, 2 * size), F32),
            VMEM((n_recv, size // 2, 2 * size), F32),
            VMEM((blocks - 1, leaves // blocks, size // 2, 2 * size), BF16),
            VMEM((blocks - 1, leaves // blocks, size // 2, 2 * size), BF16),
            pltpu.SemaphoreType.DMA((8,)),
            pltpu.SemaphoreType.DMA((5,)),
            pltpu.SemaphoreType.DMA((n_recv,)),
            pltpu.SemaphoreType.DMA((n_recv,)),
            pltpu.SemaphoreType.DMA((2,)),
            pltpu.SemaphoreType.DMA((2,)),
            pltpu.SemaphoreType.DMA((blocks - 1,)),
            pltpu.SemaphoreType.DMA((blocks - 1,)),
        ],
        compiler_params=pltpu.CompilerParams(
            collective_id=0, has_side_effects=True, vmem_limit_bytes=60 * 2**20
        ),
    )(
        leaf_pairing,
        leaf_basis,
        leaf_transfer,
        inner_transfer[0],
        jnp.transpose(upper_transfer, (1, 2, 0)),
        coupling,
        source_cluster_index.T,
        coupling_slot_mask.T,
    )

    upper_factor, q, inner_factor, projected, row_weight = pl.pallas_call(
        last_kernel,
        out_shape=(upper_shape, q_shape, inner_shape, projected_shape, weight_shape),
        in_specs=[anywhere] * 5,
        out_specs=(vmem,) + (anywhere,) * 4,
        scratch_shapes=[
            VMEM(upper_shape.shape, F32),
            VMEM(q_shape.shape, BF16),
            VMEM(inner_shape.shape, F32),
            VMEM(coupling.shape, BF16),
            VMEM(weight_shape.shape, F32),
            VMEM((2, size, 2 * size), F32),
            VMEM((2, size, 2 * size), F32),
            pltpu.SemaphoreType.DMA,
            pltpu.SemaphoreType.DMA((4,)),
            pltpu.SemaphoreType.DMA((4,)),
        ],
        compiler_params=pltpu.CompilerParams(vmem_limit_bytes=60 * 2**20),
    )(upper_gram, q, inner_factor, projected, row_weight)
    return (q, inner_factor[None], upper_factor[None], projected, row_weight)


def solution(mesh):
    placed = (
        P("leaf", None, None),
        P("leaf", None),
        P("leaf", None, None),
        P("leaf", None, None, None),
        P(),
        P("leaf", "blk", None, None),
        P("leaf", "blk"),
        P("leaf", "blk"),
    )
    return jax.shard_map(
        local,
        mesh=mesh,
        in_specs=placed,
        out_specs=(
            P("leaf", None, "blk"),
            P("leaf", None, None, None),
            P("leaf", None, None, None),
            P("leaf", "blk", None, None),
            P(("leaf", "blk"), None, None),
        ),
        check_vma=False,
    )
```

```python
import functools
import math

import jax
import jax.numpy as jnp
from jax import lax
from jax.experimental import pallas as pl
from jax.experimental.pallas import tpu as pltpu
from jax.sharding import PartitionSpec as P

F32 = jnp.float32
BF16 = jnp.bfloat16
VMEM = pltpu.VMEM
SMEM = pltpu.SMEM


def split(x):
    high = x.astype(BF16)
    return high, (x - high.astype(F32)).astype(BF16)


def dot_nn(a, b):
    return lax.dot_general(a, b, (((1,), (0,)), ((), ())), preferred_element_type=F32)


def dot_nt(a, b):
    return lax.dot_general(a, b, (((1,), (1,)), ((), ())), preferred_element_type=F32)


def dot_tn(a, b):
    return lax.dot_general(a, b, (((0,), (0,)), ((), ())), preferred_element_type=F32)


def carry(move, gram):
    move_h, move_l = move
    gram_h, gram_l = split(gram)
    right = dot_nn(gram_h, move_h) + dot_nn(gram_l, move_h)
    if move_l is not None:
        right = right + dot_nn(gram_h, move_l)
    right_h, right_l = split(right)
    out = dot_tn(move_h, right_h) + dot_tn(move_h, right_l)
    if move_l is not None:
        out = out + dot_tn(move_l, right_h)
    return out


def panel_chain(panel, start):
    count, rows, _ = panel.shape
    sub = lax.broadcasted_iota(jnp.int32, (1, rows, 128), 1)
    scale = jnp.zeros((count, rows, 128), F32)
    for r in range(rows):
        col = jnp.broadcast_to(panel[:, :, start + r : start + r + 1], panel.shape)
        inv = lax.rsqrt(col[:, r : r + 1, :])
        outer = jnp.where(sub > r, col, 0.0) * panel[:, r : r + 1, :]
        panel = panel - outer * (inv * inv)
        scale = jnp.where(sub == r, inv, scale)
    return panel * scale


def panel_ahead(panel, start):
    count, rows, _ = panel.shape
    sub = lax.broadcasted_iota(jnp.int32, (1, rows, 128), 1)
    scale = jnp.zeros((count, rows, 128), F32)
    cols = [
        jnp.broadcast_to(panel[:, :, start + r : start + r + 1], panel.shape) for r in range(rows)
    ]
    for r in range(rows):
        inv = lax.rsqrt(cols[r][:, r : r + 1, :])
        mult = jnp.where(sub > r, cols[r], 0.0) * (inv * inv)
        panel = panel - mult * panel[:, r : r + 1, :]
        for t in range(r + 1, rows):
            cols[t] = cols[t] - mult * cols[t][:, r : r + 1, :]
        scale = jnp.where(sub == r, inv, scale)
    return panel * scale


def factor_panel(work, done, first, count, rows, k, eliminate):
    size = work.shape[1]
    last = first + count
    panel = eliminate(work[first:last, k : k + rows, :], k)
    done[first:last, k : k + rows, :] = panel
    if k + rows < size:
        high, low = split(panel)
        left = jnp.concatenate([high, low, high], axis=1)
        right = jnp.concatenate([high, high, low], axis=1)
        for i in range(count):
            down = dot_tn(left[i], right[i])
            work[first + i, k + rows : size, :] = (
                work[first + i, k + rows : size, :] - down[k + rows : size, :]
            )


def upper_mask(size):
    return lax.broadcasted_iota(jnp.int32, (size, size), 0) <= lax.broadcasted_iota(
        jnp.int32, (size, size), 1
    )


def eye(size):
    return (
        lax.broadcasted_iota(jnp.int32, (size, size), 0)
        == lax.broadcasted_iota(jnp.int32, (size, size), 1)
    ).astype(F32)


def pack(matrix):
    half = matrix.shape[0] // 2
    return jnp.concatenate([matrix[:half], matrix[half:]], axis=1)


def unpack(packed):
    half = packed.shape[1] // 2
    return jnp.concatenate([packed[:, :half], packed[:, half:]], axis=0)


def tree_kernel(
    pairing_hbm,
    basis_hbm,
    leaf_move_hbm,
    inner_move_hbm,
    table_hbm,
    coupling_hbm,
    index_hbm,
    mask_hbm,
    q_hbm,
    inner_hbm,
    gram_hbm,
    projected_hbm,
    weight_hbm,
    q_out,
    inner_out,
    gram_out,
    projected,
    weight_out,
    pairing,
    basis,
    leaf_move,
    inner_move,
    table,
    moves,
    path,
    coupling,
    index,
    mask,
    work,
    done,
    extended,
    packed,
    half_ref,
    squares,
    send,
    recv,
    row_send,
    row_recv,
    in_sem,
    out_sem,
    send_sem,
    recv_sem,
    halo_send_sem,
    halo_recv_sem,
    row_send_sem,
    row_recv_sem,
):
    leaves, size, panels = basis.shape
    inner = inner_move.shape[0]
    slots = coupling.shape[1]
    part = q_out.shape[2]
    halo = leaves // 2
    n_leaf, blocks = lax.axis_size("leaf"), lax.axis_size("blk")
    me, blk = lax.axis_index("leaf"), lax.axis_index("blk")
    after, before = lax.rem(me + 1, n_leaf), lax.rem(me + n_leaf - 1, n_leaf)
    depth = gram_out.shape[0]

    loads = []
    for j, (source, target) in enumerate(
        (
            (basis_hbm, basis),
            (pairing_hbm, pairing),
            (leaf_move_hbm, leaf_move),
            (inner_move_hbm, inner_move),
            (table_hbm, table),
            (coupling_hbm, coupling),
            (index_hbm, index),
            (mask_hbm, mask),
        )
    ):
        load = pltpu.make_async_copy(source, target, in_sem.at[j])
        load.start()
        loads.append(load)

    stores = []

    def store_out(source, target):
        store = pltpu.make_async_copy(source, target, out_sem.at[len(stores)])
        store.start()
        stores.append(store)

    def flipped(apart):
        out, bit = me, 1
        while bit <= apart:
            if apart & bit:
                out = out + bit - 2 * bit * lax.rem(out // bit, 2)
            bit *= 2
        return out

    groups = [(1,)] + [(2 << (2 * g), 4 << (2 * g), 6 << (2 * g)) for g in range((depth - 1) // 2)]
    barrier = pltpu.get_barrier_semaphore()
    total = 0
    for group in groups:
        for apart in group:
            pl.semaphore_signal(barrier, 1, device_id={"leaf": flipped(apart)})
            total += 1
    for peer in (after, before):
        pl.semaphore_signal(barrier, 1, device_id={"leaf": peer})
        total += 1
    for d in range(1, blocks):
        pl.semaphore_signal(barrier, 1, device_id={"blk": lax.rem(blk + d, blocks)})
        total += 1

    used = [0, 0]

    def start_exchange(step, terms):
        firsts = []
        for term in terms:
            send[used[0]] = pack(term)
            firsts.append(used[0])
            used[0] += 1
        started = []
        for j, apart in enumerate(groups[step]):
            parts = firsts if j == 0 else firsts[-1:]
            for source in parts:
                at = used[1]
                used[1] += 1
                copy = pltpu.make_async_remote_copy(
                    src_ref=send.at[source],
                    dst_ref=recv.at[at],
                    send_sem=send_sem.at[at],
                    recv_sem=recv_sem.at[at],
                    device_id={"leaf": flipped(apart)},
                )
                copy.start()
                started.append((copy, source, at))
        return started

    def finish_exchange(started):
        sums = {}
        for copy, source, at in started:
            copy.wait_recv()
            sums[source] = sums.get(source, send[source]) + recv[at]
        return [unpack(sums[s]) for s in sorted(sums)]

    grams, going = [], []

    def advance():
        grams.extend(finish_exchange(going[-1]))
        if len(going) < len(groups):
            at = 3 * (len(going) - 1)
            terms = [
                carry((path[at], None), grams[-1]),
                carry((path[at + 1], path[at + 2]), grams[-1]),
            ]
            going.append(start_exchange(len(going), terms))

    identity = eye(size)
    for i in range(leaves + inner):
        work[i, :, size : 2 * size] = identity
    loads[0].wait()
    for i in range(leaves):
        work[i, :, 0:size] = dot_nt(basis[i], basis[i])
    for j in (1, 2, 3):
        loads[j].wait()
    for m in range(leaves // 2):
        a, b = pairing[0, 2 * m], pairing[0, 2 * m + 1]
        work[leaves + m, :, 0:size] = carry(split(leaf_move[a]), work[a, :, 0:size]) + carry(
            split(leaf_move[b]), work[b, :, 0:size]
        )
    below, count = 0, leaves // 2
    while count > 1:
        for m in range(count // 2):
            a = below + 2 * m
            work[leaves + below + count + m, :, 0:size] = carry(
                split(inner_move[a]), work[leaves + a, :, 0:size]
            ) + carry(split(inner_move[a + 1]), work[leaves + a + 1, :, 0:size])
        below, count = below + count, count // 2
    root = carry(split(inner_move[inner - 1]), work[leaves + inner - 1, :, 0:size])
    pl.semaphore_wait(barrier, total)
    going.append(start_exchange(0, [root]))
    for j in (4, 5, 6, 7):
        loads[j].wait()
    level = lax.broadcasted_iota(jnp.int32, (8, n_leaf), 0)
    column = lax.broadcasted_iota(jnp.int32, (8, n_leaf), 1)
    choose = jnp.zeros((8, n_leaf), F32)
    for j in range(1, depth):
        owner = me // (1 << j) * (1 << j) + (1 << (j - 1))
        choose = jnp.where((level == j - 1) & (column == owner), 1.0, choose)
    choose = choose.astype(BF16)
    for b in range(size // 2):
        both = jnp.concatenate([table[b], table[size // 2 + b]], axis=0)
        moves[:, b, :] = dot_nt(choose, both)[: depth - 1]
    for j in range(len(groups) - 1):
        near = unpack(moves[2 * j]).astype(BF16)
        path[3 * j] = near
        far_h, far_l = split(dot_nn(near, unpack(moves[2 * j + 1]).astype(BF16)))
        path[3 * j + 1] = far_h
        path[3 * j + 2] = far_l

    rows = 16
    for k in range(0, size, rows):
        factor_panel(work, done, 0, leaves + inner, rows, k, panel_chain)
        if k < 2 * rows:
            advance()

    keep = upper_mask(size)
    for i in range(leaves):
        low = jnp.where(keep, done[i, :, 0:size], 0.0)
        extended[halo + i] = low.astype(BF16)
        packed[halo + i] = pack(low).astype(BF16)
    halo_copies = []
    for j, (peer, source, target) in enumerate(((after, leaves, 0), (before, halo, halo + leaves))):
        copy = pltpu.make_async_remote_copy(
            src_ref=packed.at[pl.ds(source, halo)],
            dst_ref=packed.at[pl.ds(target, halo)],
            send_sem=halo_send_sem.at[j],
            recv_sem=halo_recv_sem.at[j],
            device_id={"leaf": peer},
        )
        copy.start()
        halo_copies.append(copy)

    for t in range(leaves):
        for s in range(slots):
            half_ref[t, s] = dot_nn(extended[halo + t], coupling[t, s]).astype(BF16)
    begin = pl.multiple_of(blk * part, part)
    for i in range(leaves):
        weights = (math.sqrt(panels) * done[i, :, size : 2 * size]).astype(BF16)
        q_out[i] = dot_nn(weights, basis[i, :, pl.ds(begin, part)]).astype(BF16)
    for i in range(inner):
        inner_out[i] = jnp.where(keep, done[leaves + i, :, 0:size], 0.0)
    store_out(q_out, q_hbm)
    store_out(inner_out, inner_hbm)

    advance()
    for copy in halo_copies:
        copy.wait_recv()
    for i in range(halo):
        extended[i] = unpack(packed[i])
        extended[halo + leaves + i] = unpack(packed[halo + leaves + i])
    per = leaves // blocks
    base = me * leaves - halo
    row_scale = 1.0 / (slots * blocks * size)
    row_copies = []
    for d in range(1, blocks + 1):
        peer = lax.rem(blk + d, blocks)
        for i in range(per):
            t = peer * per + i
            square = None
            for s in range(slots):
                source = jnp.clip(index[s, t] - base, 0, leaves + 2 * halo - 1)
                full = dot_nt(half_ref[t, s], extended[source])
                value = (full * mask[s, t].astype(F32)).astype(BF16)
                projected[t, s] = value
                term = dot_nt(value, value)
                square = term if square is None else square + term
            squares[d - 1, i] = square * row_scale
        if d < blocks:
            for i in range(per):
                row_send[d - 1, i] = pack(squares[d - 1, i]).astype(BF16)
            copy = pltpu.make_async_remote_copy(
                src_ref=row_send.at[d - 1],
                dst_ref=row_recv.at[d - 1],
                send_sem=row_send_sem.at[d - 1],
                recv_sem=row_recv_sem.at[d - 1],
                device_id={"blk": peer},
            )
            copy.start()
            row_copies.append(copy)
    store_out(projected, projected_hbm)
    early = len(grams)
    for i in range(early):
        work[i, :, 0:size] = grams[i]
        work[i, :, size : 2 * size] = jnp.zeros((size, size), F32)
    rows = 8
    for k in range(0, size, rows):
        factor_panel(work, done, 0, early, rows, k, panel_ahead)
    for i in range(early):
        gram_out[i] = jnp.where(keep, done[i, :, 0:size], 0.0)
    advance()
    for i in range(early, depth):
        gram_out[i] = grams[i]
    store_out(gram_out, gram_hbm)
    for copy in row_copies:
        copy.wait_recv()
    for i in range(per):
        square = row_recv[0, i].astype(F32)
        for d in range(1, blocks - 1):
            square = square + row_recv[d, i].astype(F32)
        weight_out[i] = squares[blocks - 1, i] + unpack(square)
    store_out(weight_out, weight_hbm)
    for started in going:
        for copy, _, _ in started:
            copy.wait_send()
    for copy in halo_copies + row_copies:
        copy.wait_send()
    for store in stores:
        store.wait()


def last_kernel(
    gram_hbm,
    q,
    inner,
    projected,
    weight,
    upper_out,
    q_out,
    inner_out,
    projected_out,
    weight_out,
    gram,
    q_held,
    inner_held,
    projected_held,
    weight_held,
    work,
    done,
    gram_sem,
    in_sem,
    out_sem,
):
    depth, size, _ = gram.shape
    first = pltpu.make_async_copy(gram_hbm, gram, gram_sem)
    first.start()
    loads, stores = [], []
    for j, (source, held, target) in enumerate(
        (
            (projected, projected_held, projected_out),
            (q, q_held, q_out),
            (inner, inner_held, inner_out),
            (weight, weight_held, weight_out),
        )
    ):
        loads.append(pltpu.make_async_copy(source, held, in_sem.at[j]))
        stores.append(pltpu.make_async_copy(held, target, out_sem.at[j]))
        loads[-1].start()
    first.wait()
    late = work.shape[0]
    for i in range(depth - late):
        upper_out[i] = gram[i]
    for i in range(late):
        work[i, :, 0:size] = gram[depth - late + i]
        work[i, :, size : 2 * size] = jnp.zeros((size, size), F32)
    rows = 16
    for k in range(0, size, rows):
        factor_panel(work, done, 0, late, rows, k, panel_ahead)
        if k == rows:
            for load, store in zip(loads, stores):
                load.wait()
                store.start()
    keep = upper_mask(size)
    for i in range(late):
        upper_out[depth - late + i] = jnp.where(keep, done[i, :, 0:size], 0.0)
    for store in stores:
        store.wait()


def local(
    leaf_basis,
    leaf_pairing,
    leaf_transfer,
    inner_transfer,
    upper_transfer,
    coupling,
    source_cluster_index,
    coupling_slot_mask,
):
    leaves, size, panels = leaf_basis.shape
    inner = inner_transfer.shape[1]
    n_leaf, blocks = lax.axis_size("leaf"), lax.axis_size("blk")
    depth = n_leaf.bit_length() - 1
    slots = coupling.shape[1]
    part = panels // blocks
    vmem = pl.BlockSpec(memory_space=VMEM)
    anywhere = pl.BlockSpec(memory_space=pl.ANY)

    n_recv = 1 + 4 * ((depth - 1) // 2)
    n_send = 1 + 2 * ((depth - 1) // 2)
    q_shape = jax.ShapeDtypeStruct((leaves, size, part), BF16)
    inner_shape = jax.ShapeDtypeStruct((inner, size, size), F32)
    upper_shape = jax.ShapeDtypeStruct((depth, size, size), F32)
    projected_shape = jax.ShapeDtypeStruct(coupling.shape, BF16)
    weight_shape = jax.ShapeDtypeStruct((leaves // blocks, size, size), F32)
    q, inner_factor, upper_gram, projected, row_weight = pl.pallas_call(
        tree_kernel,
        out_shape=(q_shape, inner_shape, upper_shape, projected_shape, weight_shape),
        in_specs=[anywhere] * 8,
        out_specs=(anywhere,) * 5,
        scratch_shapes=[
            VMEM(q_shape.shape, BF16),
            VMEM(inner_shape.shape, F32),
            VMEM(upper_shape.shape, F32),
            VMEM(coupling.shape, BF16),
            VMEM(weight_shape.shape, F32),
            SMEM((1, leaves), jnp.int32),
            VMEM((leaves, size, panels), BF16),
            VMEM((leaves, size, size), F32),
            VMEM((inner, size, size), F32),
            VMEM((size, size, n_leaf), BF16),
            VMEM((depth - 1, size // 2, 2 * size), F32),
            VMEM((3 * ((depth - 1) // 2), size, size), BF16),
            VMEM(coupling.shape, BF16),
            SMEM((slots, leaves), jnp.int32),
            SMEM((slots, leaves), jnp.int32),
            VMEM((leaves + inner, size, 2 * size), F32),
            VMEM((leaves + inner, size, 2 * size), F32),
            VMEM((2 * leaves, size, size), BF16),
            VMEM((2 * leaves, size // 2, 2 * size), BF16),
            VMEM((leaves, slots, size, size), BF16),
            VMEM((blocks, leaves // blocks, size, size), F32),
            VMEM((n_send, size // 2, 2 * size), F32),
            VMEM((n_recv, size // 2, 2 * size), F32),
            VMEM((blocks - 1, leaves // blocks, size // 2, 2 * size), BF16),
            VMEM((blocks - 1, leaves // blocks, size // 2, 2 * size), BF16),
            pltpu.SemaphoreType.DMA((8,)),
            pltpu.SemaphoreType.DMA((5,)),
            pltpu.SemaphoreType.DMA((n_recv,)),
            pltpu.SemaphoreType.DMA((n_recv,)),
            pltpu.SemaphoreType.DMA((2,)),
            pltpu.SemaphoreType.DMA((2,)),
            pltpu.SemaphoreType.DMA((blocks - 1,)),
            pltpu.SemaphoreType.DMA((blocks - 1,)),
        ],
        compiler_params=pltpu.CompilerParams(
            collective_id=0, has_side_effects=True, vmem_limit_bytes=60 * 2**20
        ),
    )(
        leaf_pairing,
        leaf_basis,
        leaf_transfer,
        inner_transfer[0],
        jnp.transpose(upper_transfer, (1, 2, 0)),
        coupling,
        source_cluster_index.T,
        coupling_slot_mask.T,
    )

    upper_factor, q, inner_factor, projected, row_weight = pl.pallas_call(
        last_kernel,
        out_shape=(upper_shape, q_shape, inner_shape, projected_shape, weight_shape),
        in_specs=[anywhere] * 5,
        out_specs=(vmem,) + (anywhere,) * 4,
        scratch_shapes=[
            VMEM(upper_shape.shape, F32),
            VMEM(q_shape.shape, BF16),
            VMEM(inner_shape.shape, F32),
            VMEM(coupling.shape, BF16),
            VMEM(weight_shape.shape, F32),
            VMEM((2, size, 2 * size), F32),
            VMEM((2, size, 2 * size), F32),
            pltpu.SemaphoreType.DMA,
            pltpu.SemaphoreType.DMA((4,)),
            pltpu.SemaphoreType.DMA((4,)),
        ],
        compiler_params=pltpu.CompilerParams(vmem_limit_bytes=60 * 2**20),
    )(upper_gram, q, inner_factor, projected, row_weight)
    return (q, inner_factor[None], upper_factor[None], projected, row_weight)


def solution(mesh):
    placed = (
        P("leaf", None, None),
        P("leaf", None),
        P("leaf", None, None),
        P("leaf", None, None, None),
        P(),
        P("leaf", "blk", None, None),
        P("leaf", "blk"),
        P("leaf", "blk"),
    )
    return jax.shard_map(
        local,
        mesh=mesh,
        in_specs=placed,
        out_specs=(
            P("leaf", None, "blk"),
            P("leaf", None, None, None),
            P("leaf", None, None, None),
            P("leaf", "blk", None, None),
            P(("leaf", "blk"), None, None),
        ),
        check_vma=False,
    )
```
